32 devices in a mesh: shard: 4 (over z), ctx: 2 (over x), tensor: 4 (over y, core).
Axes of the slice: x: 2, y: 2, z: 4, core: 2. Of those that a mesh axis runs over, the one named last changes fastest.
Arguments:
- tokens: bfloat16 [4096, 1024], P(('shard', 'ctx')), may hold values from -6 to 6
- cotangent: bfloat16 [4096, 1024], P(('shard', 'ctx')), may hold values from -6 to 6
- lengths: int32 [4], P('shard'), may hold values from 640 to 1024, as said below
- qkv_weight: float32 [3, 1024, 1024], P(None, ('shard', 'ctx'), 'tensor'), may hold values from -0.1875 to 0.1875
- out_weight: float32 [1024, 1024], P('tensor', ('shard', 'ctx')), may hold values from -0.375 to 0.375
- up_weight: float32 [1024, 4096], P(('shard', 'ctx'), 'tensor'), may hold values from -0.1875 to 0.1875
- down_weight: float32 [4096, 1024], P('tensor', ('shard', 'ctx')), may hold values from -0.09375 to 0.09375
- vectors: float32 [12288], P(('shard', 'ctx', 'tensor')), may hold values from -1.2 to 1.45
- qkv_first: float32 [3, 1024, 1024], P(None, ('shard', 'ctx'), 'tensor'), may hold values from -4 to 4
- out_first: float32 [1024, 1024], P('tensor', ('shard', 'ctx')), may hold values from -12 to 12
- up_first: float32 [1024, 4096], P(('shard', 'ctx'), 'tensor'), may hold values from -10 to 10
- down_first: float32 [4096, 1024], P('tensor', ('shard', 'ctx')), may hold values from -20 to 20
- vec_first: float32 [12288], P(('shard', 'ctx', 'tensor')), may hold values from -20 to 20
- qkv_second: float32 [3, 1024, 1024], P(None, ('shard', 'ctx'), 'tensor'), may hold values from 1.06496 to 17.2032
- out_second: float32 [1024, 1024], P('tensor', ('shard', 'ctx')), may hold values from 9.8304 to 155.648
- up_second: float32 [1024, 4096], P(('shard', 'ctx'), 'tensor'), may hold values from 6.5536 to 106.496
- down_second: float32 [4096, 1024], P('tensor', ('shard', 'ctx')), may hold values from 27.0336 to 430.08
- vec_second: float32 [12288], P(('shard', 'ctx', 'tensor')), may hold values from 27.0336 to 430.08
Outputs:
- layer_out: bfloat16 [4096, 1024], P(('shard', 'ctx', 'tensor'))
- token_grad: float32 [4096, 1024], P(('shard', 'ctx', 'tensor'))
- qkv_moment: float32 [3, 1024, 1024], P(None, ('shard', 'ctx'), 'tensor')
- out_moment: float32 [1024, 1024], P('tensor', ('shard', 'ctx'))
- up_moment: float32 [1024, 4096], P(('shard', 'ctx'), 'tensor')
- down_moment: float32 [4096, 1024], P('tensor', ('shard', 'ctx'))
- vec_moment: float32 [12288], P(('shard', 'ctx', 'tensor'))
- qkv_square: float32 [3, 1024, 1024], P(None, ('shard', 'ctx'), 'tensor')
- out_square: float32 [1024, 1024], P('tensor', ('shard', 'ctx'))
- up_square: float32 [1024, 4096], P(('shard', 'ctx'), 'tensor')
- down_square: float32 [4096, 1024], P('tensor', ('shard', 'ctx'))
- vec_square: float32 [12288], P(('shard', 'ctx', 'tensor'))
- qkv_new: float32 [3, 1024, 1024], P(None, ('shard', 'ctx'), 'tensor')
- out_new: float32 [1024, 1024], P('tensor', ('shard', 'ctx'))
- up_new: float32 [1024, 4096], P(('shard', 'ctx'), 'tensor')
- down_new: float32 [4096, 1024], P('tensor', ('shard', 'ctx'))
- vec_new: float32 [12288], P(('shard', 'ctx', 'tensor'))
The draws below stay inside these ranges and needn't reach their ends.
Inputs may be any that keep to these rules, and one draw needn't show every extreme that they name: lengths[s] tokens at the head of sequence s are live, the other rows of its slot are padding; some sequence has all 1024.
All inputs are finite; a program needn't handle non-finite values.
Results may differ from the reference program's by a relative error of at most 0.011.
The reference program's roundings to bfloat16 on the way count: a program that leaves them out, or rounds other values in their place, can miss the bound.
Values may be sent and summed in bfloat16 or wider, within the bound.
No kernel may reach another device: no remote copies, remote signals or barrier semaphores. Data moves between devices by JAX's collectives and lax.ppermute only.
A program may use at most 128 MiB of HBM per device.

```python
import math
import jax
import jax.numpy as jnp
from jax import lax

D = 1024
HEADS = 16
HDIM = 64
FF = 4096
TOK_DEV = 512
STEP = 10
SEQ = 1024
GROUPS = 4
TOKENS = 4096
VEC = 12288


def draw_lengths(key, part):
    key = jax.random.fold_in(key, 11)
    key_one, key_two = jax.random.split(key)
    shortest = TOK_DEV + TOK_DEV // 4
    longest = SEQ
    drawn_len = jax.random.randint(key_one, (GROUPS,), shortest, longest + 1)
    full_group = jax.random.randint(key_two, (), 0, GROUPS)
    return jnp.where(jnp.arange(GROUPS) == full_group, longest, drawn_len).astype(jnp.int32)


def draw_vectors(key, part):
    key = jax.random.fold_in(key, 5)
    section = jnp.arange(VEC) // D
    is_gain = (section == 0) | (section == 5)
    noise_draw = jax.random.normal(key, (VEC,), jnp.float32)
    gains = 1.0 + 0.15 * jnp.clip(noise_draw, -3.0, 3.0)
    shifts = 0.3 * jnp.clip(noise_draw, -4.0, 4.0)
    return jnp.where(is_gain, gains, shifts).astype(jnp.float32)


def steps_of(key, extent, cuts, least, high):
    def one(axis_at, parts):
        draws = jax.random.uniform(jax.random.fold_in(jax.random.fold_in(key, 6), axis_at), (parts,), jnp.float32, least / len(cuts), high / len(cuts))
        return jnp.repeat(jnp.exp(draws), extent[axis_at] // parts).reshape((-1,) + (1,) * (len(extent) - axis_at - 1))

    loudness = one(*cuts[0])
    for cut in cuts[1:]:
        loudness = loudness * one(*cut)
    return loudness


def scatter_about(key, dims, spread, bound, pieces=(), dtype=jnp.bfloat16):
    level = steps_of(key, dims, pieces, -0.22, 0.18) if pieces else 1.0
    entries = jax.random.normal(key, dims, jnp.float32) * spread * level
    return jnp.minimum(jnp.maximum(entries, -bound), bound).astype(dtype)


def setup_inputs(seed: int = 0) -> dict:
    seeds = jax.random.split(jax.random.key(seed), 19)
    tokens = scatter_about(seeds[0], (TOKENS, D), 1.0, 6.0, ((0, 8),))
    cotangent = scatter_about(seeds[1], (TOKENS, D), 1.0, 6.0, ((0, 8),))
    lengths = draw_lengths(jax.random.fold_in(seeds[18], 71), 0)
    qkv_weight = scatter_about(seeds[3], (3, D, D), D ** -0.5, 0.1875, ((1, 8), (2, 4)), jnp.float32)
    out_weight = scatter_about(seeds[4], (D, D), (D // 4) ** -0.5, 0.375, ((0, 4), (1, 8)), jnp.float32)
    up_weight = scatter_about(seeds[5], (D, FF), D ** -0.5, 0.1875, ((0, 8), (1, 4)), jnp.float32)
    down_weight = scatter_about(seeds[6], (FF, D), FF ** -0.5, 0.09375, ((0, 4), (1, 8)), jnp.float32)
    vectors = draw_vectors(jax.random.fold_in(seeds[18], 71), 0)
    qkv_first = scatter_about(seeds[8], (3, D, D), (0.0111 * TOKENS ** 0.5), 4.0, ((1, 8), (2, 4)), jnp.float32)
    out_first = scatter_about(seeds[9], (D, D), (0.033 * TOKENS ** 0.5), 12.0, ((0, 4), (1, 8)), jnp.float32)
    up_first = scatter_about(seeds[10], (D, FF), (0.028 * TOKENS ** 0.5), 10.0, ((0, 8), (1, 4)), jnp.float32)
    down_first = scatter_about(seeds[11], (FF, D), (0.055 * TOKENS ** 0.5), 20.0, ((0, 4), (1, 8)), jnp.float32)
    vec_first = scatter_about(seeds[12], (VEC,), (0.055 * TOKENS ** 0.5), 20.0, ((0, 32),), jnp.float32)
    qkv_second = jnp.clip(jnp.exp(math.log(17.2032) - 2.7821581 * jax.random.uniform(seeds[13], (3, D, D), jnp.float32) ** steps_of(seeds[13], (3, D, D), ((1, 8), (2, 4)), -0.2, 0.2)), 1.06496, 17.2032)
    out_second = jnp.clip(jnp.exp(math.log(155.648) - 2.7621173 * jax.random.uniform(seeds[14], (D, D), jnp.float32) ** steps_of(seeds[14], (D, D), ((0, 4), (1, 8)), -0.2, 0.2)), 9.8304, 155.648)
    up_second = jnp.clip(jnp.exp(math.log(106.496) - 2.78809295 * jax.random.uniform(seeds[15], (D, FF), jnp.float32) ** steps_of(seeds[15], (D, FF), ((0, 8), (1, 4)), -0.2, 0.2)), 6.5536, 106.496)
    down_second = jnp.clip(jnp.exp(math.log(430.08) - 2.7668907 * jax.random.uniform(seeds[16], (FF, D), jnp.float32) ** steps_of(seeds[16], (FF, D), ((0, 4), (1, 8)), -0.2, 0.2)), 27.0336, 430.08)
    vec_second = jnp.clip(jnp.exp(math.log(430.08) - 2.7668907 * jax.random.uniform(seeds[17], (VEC,), jnp.float32) ** steps_of(seeds[17], (VEC,), ((0, 32),), -0.2, 0.2)), 27.0336, 430.08)
    return dict(tokens=tokens, cotangent=cotangent, lengths=lengths, qkv_weight=qkv_weight, out_weight=out_weight, up_weight=up_weight, down_weight=down_weight, vectors=vectors, qkv_first=qkv_first, out_first=out_first, up_first=up_first, down_first=down_first, vec_first=vec_first, qkv_second=qkv_second, out_second=out_second, up_second=up_second, down_second=down_second, vec_second=vec_second)


@jax.custom_vjp
def low(v):
    return lax.optimization_barrier(v.astype(jnp.bfloat16)).astype(jnp.float32)

@jax.custom_vjp
def low_back(v):
    return v

def low_keep(v):
    return (low(v), None)

def low_pass(kept, grad):
    return (grad,)

def back_keep(v):
    return (v, None)

def back_low(kept, grad):
    return (low(grad),)
low.defvjp(low_keep, low_pass)
low_back.defvjp(back_keep, back_low)
highest = lax.Precision.HIGHEST
norm_eps = 1e-05
mask_value = -1e+30
beta_first = 0.9
beta_second = 0.95
adam_eps = 1e-08
decay_coef = 0.1
rate_matrix = 0.05
rate_vector = 0.6

def layer_norm(values, gain_vec, shift_vec):
    row_mean = lax.optimization_barrier(jnp.mean(values, axis=-1, keepdims=True))
    centred = values - row_mean
    row_var = lax.optimization_barrier(jnp.mean(centred * centred, axis=-1, keepdims=True))
    return centred * lax.rsqrt(row_var + norm_eps) * gain_vec + shift_vec

def gelu_tanh(values):
    return 0.5 * values * (1.0 + jnp.tanh(0.7978845608028654 * (values + 0.044715 * values * values * values)))

def alibi_slopes():
    return jnp.exp2(-8.0 * (jnp.arange(HEADS).astype(jnp.float32) + 1.0) / HEADS)

def group_layer(group_rows, qkv_low, out_low, up_low, down_low, vectors):
    seq_rows = group_rows.shape[0]
    gain_one = vectors[0:D]
    shift_one = vectors[D:2 * D]
    bias_query = vectors[2 * D:3 * D]
    bias_value = vectors[3 * D:4 * D]
    bias_out = vectors[4 * D:5 * D]
    gain_two = vectors[5 * D:6 * D]
    shift_two = vectors[6 * D:7 * D]
    bias_down = vectors[7 * D:8 * D]
    bias_up = vectors[8 * D:8 * D + FF]
    normed_one = low(layer_norm(group_rows, gain_one, shift_one))
    query_rows = low_back(low(jnp.dot(normed_one, qkv_low[0], precision=highest) + bias_query))
    key_rows = low_back(low(jnp.dot(normed_one, qkv_low[1], precision=highest)))
    value_rows = low_back(low(jnp.dot(normed_one, qkv_low[2], precision=highest) + bias_value))
    query_heads = query_rows.reshape(seq_rows, HEADS, HDIM)
    key_heads = key_rows.reshape(seq_rows, HEADS, HDIM)
    value_heads = value_rows.reshape(seq_rows, HEADS, HDIM)
    positions = jnp.arange(seq_rows)
    offset = (positions[None, :] - positions[:, None]).astype(jnp.float32)
    scores = jnp.einsum('qhd,khd->hqk', query_heads, key_heads, precision=highest) * HDIM ** (-0.5)
    scores = low_back(scores + alibi_slopes()[:, None, None] * offset[None])
    causal = positions[None, :] <= positions[:, None]
    masked = jnp.where(causal[None], scores, mask_value)
    row_top = lax.optimization_barrier(jnp.max(masked, axis=-1, keepdims=True))
    exp_scores = jnp.exp(masked - row_top)
    probs_low = low(exp_scores / lax.optimization_barrier(jnp.sum(exp_scores, axis=-1, keepdims=True)))
    context = jnp.einsum('hqk,khd->qhd', probs_low, value_heads, precision=highest).reshape(seq_rows, D)
    context = low_back(low(context))
    attended = low_back(jnp.dot(context, out_low, precision=highest) + bias_out)
    hidden = group_rows + attended
    normed_two = low(layer_norm(hidden, gain_two, shift_two))
    upward = low_back(jnp.dot(normed_two, up_low, precision=highest) + bias_up)
    activated = low(gelu_tanh(upward))
    downward = low_back(jnp.dot(activated, down_low, precision=highest) + bias_down)
    return hidden + downward

def forward(tokens_f, qkv_weight, out_weight, up_weight, down_weight, vectors):
    qkv_low = low(qkv_weight)
    out_low = low(out_weight)
    up_low = low(up_weight)
    down_low = low(down_weight)

    def one_group(group_rows):
        return group_layer(group_rows, qkv_low, out_low, up_low, down_low, vectors)
    results = lax.map(jax.checkpoint(one_group), tokens_f.reshape(GROUPS, SEQ, D))
    return results.reshape(GROUPS * SEQ, D)

def adam_update(weight, gradient, first_mom, second, step_rate, decay_here):
    moment = beta_first * first_mom + (1.0 - beta_first) * gradient
    square = beta_second * second + (1.0 - beta_second) * gradient * gradient
    ratio = moment / (1.0 - beta_first ** STEP) / (jnp.sqrt(square / (1.0 - beta_second ** STEP)) + adam_eps)
    new_weight = weight - step_rate * (ratio + decay_here * weight)
    return (moment, square, new_weight)

def reference(tokens, cotangent, lengths, qkv_weight, out_weight, up_weight, down_weight, vectors, qkv_first, out_first, up_first, down_first, vec_first, qkv_second, out_second, up_second, down_second, vec_second):
    tokens_f = tokens.astype(jnp.float32)
    layer_rows, pullback = jax.vjp(forward, tokens_f, qkv_weight, out_weight, up_weight, down_weight, vectors)
    live_rows = (jnp.arange(SEQ)[None, :] < lengths[:, None]).astype(jnp.float32)
    cot_rows = (cotangent.astype(jnp.float32).reshape(GROUPS, SEQ, D) * live_rows[:, :, None]).reshape(GROUPS * SEQ, D)
    gradients = pullback(cot_rows)
    qkv_moment, qkv_square, qkv_new = adam_update(qkv_weight, gradients[1], qkv_first, qkv_second, rate_matrix, decay_coef)
    out_moment, out_square, out_new = adam_update(out_weight, gradients[2], out_first, out_second, rate_matrix, decay_coef)
    up_moment, up_square, up_new = adam_update(up_weight, gradients[3], up_first, up_second, rate_matrix, decay_coef)
    down_moment, down_square, down_new = adam_update(down_weight, gradients[4], down_first, down_second, rate_matrix, decay_coef)
    vec_moment, vec_square, vec_new = adam_update(vectors, gradients[5], vec_first, vec_second, rate_vector, 0.0)
    return (layer_rows.astype(jnp.bfloat16), gradients[0], qkv_moment, out_moment, up_moment, down_moment, vec_moment, qkv_square, out_square, up_square, down_square, vec_square, qkv_new, out_new, up_new, down_new, vec_new)
```

```python
import functools

import jax
import jax.numpy as jnp
from jax import lax
from jax.experimental import pallas as pl
from jax.experimental.pallas import tpu as pltpu
from jax.sharding import PartitionSpec as P

HEADS = 16
HDIM = 64
STEP = 10
ALL = ("shard", "ctx", "tensor")
PLANE = ("ctx", "tensor")

norm_eps = 1e-05
mask_value = -1e30
beta_first = 0.9
beta_second = 0.95
adam_eps = 1e-08
decay_coef = 0.1
rate_matrix = 0.05
rate_vector = 0.6

low = jnp.bfloat16
f32 = jnp.float32


def mask_of(j):
    return ((j & 3) << 1) | (j >> 2)


def rel_of(mask):
    return ((mask & 1) << 2) | (mask >> 1)


def to_peer(value, mask):
    return lax.ppermute(value, PLANE, [(i, i ^ mask) for i in range(8)])


X_HOP, Y_HOP, XY_HOP, CORE_HOP = 4, 2, 6, 1


def along_shard(value, steps):
    count = lax.axis_size("shard")
    return lax.ppermute(value, "shard", [(i, (i + steps) % count) for i in range(count)])


def swap_ctx(value):
    return lax.ppermute(value, "ctx", [(0, 1), (1, 0)])


def gather_plane(block):
    quad = jnp.stack([block, to_peer(block, Y_HOP), to_peer(block, X_HOP), to_peer(block, XY_HOP)])
    return jnp.concatenate([quad, to_peer(quad, CORE_HOP)], axis=0)


def scatter_plane(lhs, rhs, dims):
    half = lhs.shape[0] // 2
    far = lax.dot_general(lhs[half:], rhs, (dims, ((), ())), preferred_element_type=f32).astype(low)
    got = to_peer(far, CORE_HOP)
    near = lax.dot_general(lhs[:half], rhs, (dims, ((), ())), preferred_element_type=f32)
    quad = (near + got.astype(f32)).reshape((4, half // 4) + near.shape[1:])
    quad_low = quad[1:].astype(low)
    parts = [to_peer(quad_low[0], Y_HOP), to_peer(quad_low[1], X_HOP), to_peer(quad_low[2], XY_HOP)]
    return quad[0] + parts[0].astype(f32) + parts[1].astype(f32) + parts[2].astype(f32)


def ring_gather(block, axis):
    count = lax.axis_size("shard")
    if count > 4:
        return lax.all_gather(block, "shard", axis=axis, tiled=True)
    blocks = [block]
    for _ in range(count - 1):
        blocks.append(along_shard(blocks[-1], 1))
    return jnp.concatenate(blocks, axis=axis)


def ring_scatter(whole, axis):
    count = lax.axis_size("shard")
    if count > 4:
        return lax.psum_scatter(whole, "shard", scatter_dimension=axis, tiled=True)
    blocks = jnp.split(whole, count, axis=axis)
    total = blocks[-1]
    for k in range(count - 2, -1, -1):
        total = along_shard(total.astype(low), -1).astype(f32) + blocks[k]
    return total


def turn_blocks(value, axis):
    count = lax.axis_size("shard")
    if count > 4:
        return value
    place = lax.axis_index("shard")
    size = value.shape[axis] // count
    parts = [
        lax.dynamic_slice_in_dim(value, lax.rem(place - k + count, count) * size, size, axis)
        for k in range(count)
    ]
    return jnp.concatenate(parts, axis=axis)


def in_order(first, own, other, axis):
    return jnp.where(
        first, jnp.concatenate([own, other], axis), jnp.concatenate([other, own], axis)
    )


def pick_half(first, value, axis):
    a, b = jnp.split(value, 2, axis=axis)
    return jnp.where(first, a, b), jnp.where(first, b, a)


def gather_vectors(vec):
    shards = lax.axis_size("shard")
    if shards > 4:
        return lax.all_gather(vec, ALL, axis=0, tiled=True)
    place = lax.axis_index("shard")
    rank = lax.axis_index("ctx") * 4 + lax.axis_index("tensor")
    column = jnp.stack([vec] + [along_shard(vec, k) for k in range(1, shards)])
    both = gather_plane(column).reshape(8 * shards, -1)
    at = jnp.arange(8 * shards)
    z, r = at // 8, at % 8
    index = rel_of(r ^ rank) * shards + (place - z + shards) % shards
    return jnp.take(both, index, axis=0).reshape(-1)


def scatter_vectors(term):
    shards = lax.axis_size("shard")
    if shards > 4:
        return lax.psum_scatter(term, ALL, scatter_dimension=0, tiled=True)
    place = lax.axis_index("shard")
    rank = lax.axis_index("ctx") * 4 + lax.axis_index("tensor")
    at = jnp.arange(8 * shards)
    j, k = at // shards, at % shards
    index = ((place - k + shards) % shards) * 8 + (rank ^ mask_of(j))
    rel = jnp.take(term.reshape(8 * shards, -1), index, axis=0).reshape(2, 4, shards, -1)
    quad = rel[0] + to_peer(rel[1], CORE_HOP)
    column = quad[0] + to_peer(quad[1], Y_HOP) + to_peer(quad[2], X_HOP) + to_peer(quad[3], XY_HOP)
    total = column[0]
    for k in range(1, shards):
        total = total + along_shard(column[k], -k)
    return total


def adam_update(weight, gradient, first_mom, second, step_rate, decay_here):
    moment = beta_first * first_mom + (1.0 - beta_first) * gradient
    square = beta_second * second + (1.0 - beta_second) * gradient * gradient
    ratio = (
        moment
        / (1.0 - beta_first**STEP)
        / (jnp.sqrt(square / (1.0 - beta_second**STEP)) + adam_eps)
    )
    new_weight = weight - step_rate * (ratio + decay_here * weight)
    return (moment, square, new_weight)


def norm_stats(values):
    row_mean = jnp.mean(values, axis=-1, keepdims=True)
    centred = values - row_mean
    row_var = jnp.mean(centred * centred, axis=-1, keepdims=True)
    return row_mean, lax.rsqrt(row_var + norm_eps)


def norm_back(grad, hat, scale, gain):
    scaled = grad * gain
    inner = jnp.mean(scaled * hat, axis=-1, keepdims=True)
    return scale * (scaled - jnp.mean(scaled, axis=-1, keepdims=True) - hat * inner)


BLOCK = 256


def dot_nt(a, b):
    return lax.dot_general(a, b, (((1,), (1,)), ((), ())), preferred_element_type=f32)


def dot_nn(a, b):
    return lax.dot_general(a, b, (((1,), (0,)), ((), ())), preferred_element_type=f32)


def dot_tn(a, b):
    return lax.dot_general(a, b, (((0,), (0,)), ((), ())), preferred_element_type=f32)


def block_of(rank, b):
    return pl.multiple_of(rel_of(b ^ rank) * 128, 128)


def score_pieces(nat, slope, head, at):
    lanes = pl.ds(head * HDIM, HDIM)
    query = nat[pl.ds(at * BLOCK, BLOCK), lanes] * low(HDIM**-0.5)
    pieces = []
    spans = ([(0, at * BLOCK)] if at else []) + [(at * BLOCK, BLOCK)]
    for start, size in spans:
        key = nat[pl.ds(start, size), pl.ds(128 + head * HDIM, HDIM)]
        raw = dot_nt(key, query)
        down = lax.broadcasted_iota(jnp.int32, (size, BLOCK), 0)
        raw = raw + slope * (down + (start - at * BLOCK)).astype(f32)
        if start == at * BLOCK:
            across = lax.broadcasted_iota(jnp.int32, (size, BLOCK), 1)
            raw = jnp.where(down <= across, raw, mask_value)
        pieces.append((start, size, key, raw))
    return query, pieces


def attend_kernel(rank_ref, slope_ref, qkv_ref, out_ref, top_ref, nat):
    rank = rank_ref[0]
    rows = qkv_ref.shape[0]
    for b in range(rows // 128):
        nat[pl.ds(b * 128, 128), :] = qkv_ref[pl.ds(block_of(rank, b), 128), :]
    for at in range(rows // BLOCK):
        outs = []
        for head in range(2):
            _, pieces = score_pieces(nat, slope_ref[head], head, at)
            top = functools.reduce(
                jnp.maximum, [jnp.max(raw, axis=0, keepdims=True) for _, _, _, raw in pieces]
            )
            probs = [jnp.exp(raw - top) for _, _, _, raw in pieces]
            total = sum(jnp.sum(p, axis=0, keepdims=True) for p in probs)
            inverse = 1.0 / total
            mixed = jnp.zeros((HDIM, BLOCK), f32)
            for (start, size, _, _), p in zip(pieces, probs):
                value = nat[pl.ds(start, size), pl.ds(256 + head * HDIM, HDIM)]
                mixed = mixed + dot_tn(value, (p * inverse).astype(low))
            outs.append(mixed.T)
            top_ref[pl.ds(head, 1), pl.ds(at * BLOCK, BLOCK)] = top + jnp.log(total)
        both = jnp.concatenate(outs, axis=1).astype(low)
        for part in range(BLOCK // 128):
            b = at * (BLOCK // 128) + part
            out_ref[pl.ds(block_of(rank, b), 128), :] = both[part * 128 : (part + 1) * 128]


def attend_back_kernel(rank_ref, slope_ref, qkv_ref, grad_ref, top_ref, out_ref, nat, gnat, acc):
    rank = rank_ref[0]
    rows = qkv_ref.shape[0]
    for b in range(rows // 128):
        there = pl.ds(block_of(rank, b), 128)
        nat[pl.ds(b * 128, 128), :] = qkv_ref[there, :]
        gnat[pl.ds(b * 128, 128), :] = grad_ref[there, :]
    for head in range(2):
        for at in range(rows // BLOCK - 1, -1, -1):
            here = pl.ds(at * BLOCK, BLOCK)
            query, pieces = score_pieces(nat, slope_ref[head], head, at)
            grad = gnat[here, pl.ds(head * HDIM, HDIM)]
            log_total = top_ref[pl.ds(head, 1), here]
            probs, slopes = [], []
            inner = jnp.zeros((1, BLOCK), f32)
            for start, size, _, raw in pieces:
                value = nat[pl.ds(start, size), pl.ds(256 + head * HDIM, HDIM)]
                p = jnp.exp(raw - log_total)
                d = dot_nt(value, grad)
                inner = inner + jnp.sum(p * d, axis=0, keepdims=True)
                probs.append(p)
                slopes.append(d)
            query_grad = jnp.zeros((HDIM, BLOCK), f32)
            for (start, size, key, _), p, d in zip(pieces, probs, slopes):
                s = (p * (d - inner)).astype(low)
                query_grad = query_grad + dot_tn(key, s)
                key_grad = dot_nn(s, query)
                value_grad = dot_nn(p.astype(low), grad)
                k_at = (pl.ds(start, size), pl.ds(128 + head * HDIM, HDIM))
                v_at = (pl.ds(start, size), pl.ds(256 + head * HDIM, HDIM))
                if at == rows // BLOCK - 1:
                    acc[k_at] = key_grad
                    acc[v_at] = value_grad
                else:
                    acc[k_at] += key_grad
                    acc[v_at] += value_grad
            acc[here, pl.ds(head * HDIM, HDIM)] = query_grad.T * (HDIM**-0.5)
    for b in range(rows // 128):
        out_ref[pl.ds(block_of(rank, b), 128), :] = acc[pl.ds(b * 128, 128), :].astype(low)


smem = pl.BlockSpec(memory_space=pltpu.SMEM)
vmem = pl.BlockSpec(memory_space=pltpu.VMEM)


def attend(rank, slopes, qkv):
    rows = qkv.shape[0]
    return pl.pallas_call(
        attend_kernel,
        out_shape=(
            jax.ShapeDtypeStruct((rows, 2 * HDIM), low),
            jax.ShapeDtypeStruct((8, rows), f32),
        ),
        in_specs=[smem, smem, vmem],
        out_specs=(vmem, vmem),
        scratch_shapes=[pltpu.VMEM((rows, 6 * HDIM), low)],
        compiler_params=pltpu.CompilerParams(vmem_limit_bytes=32 * 1024 * 1024),
        cost_estimate=pl.CostEstimate(
            flops=6 * rows * rows * HDIM, bytes_accessed=rows * 1100, transcendentals=rows * rows
        ),
    )(rank, slopes, qkv)


def attend_back(rank, slopes, qkv, grad, tops):
    rows = qkv.shape[0]
    return pl.pallas_call(
        attend_back_kernel,
        out_shape=jax.ShapeDtypeStruct((rows, 6 * HDIM), low),
        in_specs=[smem, smem, vmem, vmem, vmem],
        out_specs=vmem,
        scratch_shapes=[
            pltpu.VMEM((rows, 6 * HDIM), low),
            pltpu.VMEM((rows, 2 * HDIM), low),
            pltpu.VMEM((rows, 6 * HDIM), f32),
        ],
        compiler_params=pltpu.CompilerParams(vmem_limit_bytes=32 * 1024 * 1024),
        cost_estimate=pl.CostEstimate(
            flops=15 * rows * rows * HDIM, bytes_accessed=rows * 1900, transcendentals=rows * rows
        ),
    )(rank, slopes, qkv, grad, tops)


def per_device(
    tokens,
    cotangent,
    lengths,
    qkv_weight,
    out_weight,
    up_weight,
    down_weight,
    vectors,
    qkv_first,
    out_first,
    up_first,
    down_first,
    vec_first,
    qkv_second,
    out_second,
    up_second,
    down_second,
    vec_second,
):
    tok_rows, feat = tokens.shape
    ctx = lax.axis_index("ctx")
    part = lax.axis_index("tensor")
    first = ctx == 0
    rank = ctx * 4 + part
    share = tok_rows // 4
    rows = 8 * share
    width = 2 * HDIM
    hidden = up_weight.shape[1] // 2

    def fetch(weight, column_axis, feature_axis):
        own, send = pick_half(first, weight.astype(low), column_axis)
        return in_order(first, own, swap_ctx(send), feature_axis)

    qkv_flat = jnp.concatenate(
        [
            jnp.concatenate([qkv_weight[i][:, h * width : (h + 1) * width] for i in range(3)], axis=1)
            for h in range(2)
        ],
        axis=1,
    )
    qkv_block = fetch(qkv_flat, 1, 0)
    out_block = fetch(out_weight, 0, 1)
    up_block = fetch(up_weight, 1, 0)
    down_block = fetch(down_weight, 0, 1)

    tok_own = turn_blocks(lax.dynamic_slice_in_dim(tokens, part * share, share, 0), 1)
    tok_all = gather_plane(tok_own).reshape(rows, feat)
    vec_full = gather_vectors(vectors)
    qkv_low = ring_gather(qkv_block, 0)
    out_low = ring_gather(out_block, 1)

    wide = turn_blocks(vec_full[: 8 * feat].reshape(8, feat), 1)
    gain_one, shift_one, bias_out, gain_two, shift_two, bias_down = (
        wide[i] for i in (0, 1, 4, 5, 6, 7)
    )
    head_at = part * (2 * width) + ctx * width
    bias_query = lax.dynamic_slice_in_dim(vec_full, 2 * feat + head_at, width)
    bias_value = lax.dynamic_slice_in_dim(vec_full, 3 * feat + head_at, width)
    hidden_at = part * (2 * hidden) + ctx * hidden
    bias_up = lax.dynamic_slice_in_dim(vec_full, 8 * feat + hidden_at, hidden)
    bias_qkv = jnp.concatenate([bias_query, jnp.zeros((width,), f32), bias_value])

    tok_f = tok_all.astype(f32)
    mean_one, scale_one = norm_stats(tok_f)
    normed_low = ((tok_f - mean_one) * scale_one * gain_one + shift_one).astype(low)
    qkv = (jnp.dot(normed_low, qkv_low, preferred_element_type=f32) + bias_qkv).astype(low)

    up_low = ring_gather(up_block, 0)
    down_low = ring_gather(down_block, 1)
    out_full = gather_plane(out_low).reshape(8 * width, feat)

    slopes_all = jnp.exp2(-8.0 * (jnp.arange(HEADS).astype(f32) + 1.0) / HEADS)
    slopes = lax.dynamic_slice_in_dim(slopes_all, part * 4 + ctx * 2, 2)
    rank_arg = rank.astype(jnp.int32).reshape(1)
    context, tops = attend(rank_arg, slopes, qkv)

    blocks = context.reshape(2, 4, share, width)
    quad = jnp.concatenate([blocks[0], to_peer(blocks[1], CORE_HOP)], axis=2)
    quad = jnp.stack(
        [quad[0], to_peer(quad[1], Y_HOP), to_peer(quad[2], X_HOP), to_peer(quad[3], XY_HOP)]
    )
    context_rows = jnp.concatenate(
        [quad[i][:, c * width : (c + 1) * width] for c in range(2) for i in range(4)], axis=1
    )
    hidden_rows = (
        tok_own.astype(f32)
        + jnp.dot(context_rows, out_full, preferred_element_type=f32)
        + bias_out
    )
    mean_two, scale_two = norm_stats(hidden_rows)
    hat_two = (hidden_rows - mean_two) * scale_two
    normed_two = gather_plane((hat_two * gain_two + shift_two).astype(low)).reshape(rows, feat)

    own_pos = rank * share + jnp.arange(share)
    live = (own_pos < lengths[0])[:, None]
    cot_own = turn_blocks(lax.dynamic_slice_in_dim(cotangent, part * share, share, 0), 1)
    out_grad = jnp.where(live, cot_own, low(0))
    out_grad_all = gather_plane(out_grad).reshape(rows, feat)

    upward = jnp.dot(normed_two, up_low, preferred_element_type=f32) + bias_up
    act_grad = dot_nt(out_grad_all, down_low)
    coef = 0.7978845608028654
    tanh = jnp.tanh(coef * (upward + 0.044715 * upward * upward * upward))
    activated = (0.5 * upward * (1.0 + tanh)).astype(low)
    slope = 0.5 * (1.0 + tanh) + 0.5 * upward * (1.0 - tanh * tanh) * coef * (
        1.0 + 3.0 * 0.044715 * upward * upward
    )
    up_grad = (act_grad * slope).astype(low)

    norm_two_grad = scatter_plane(up_grad, up_low, ((1,), (1,)))
    down_grad_weight = dot_tn(activated, out_grad_all)
    up_grad_weight = dot_tn(normed_two, up_grad)
    down_owned = ring_scatter(down_grad_weight, 1)
    up_owned = ring_scatter(up_grad_weight, 0)

    hidden_grad = out_grad.astype(f32) + norm_back(norm_two_grad, hat_two, scale_two, gain_two)
    attn_grad = hidden_grad.astype(low)
    grad_rows = dot_nt(attn_grad, out_full).astype(low)
    pairs = [
        jnp.concatenate(
            [grad_rows[:, (c * 4 + i) * width : (c * 4 + i + 1) * width] for c in range(2)], axis=1
        )
        for i in range(4)
    ]
    quad = jnp.stack(
        [pairs[0], to_peer(pairs[1], Y_HOP), to_peer(pairs[2], X_HOP), to_peer(pairs[3], XY_HOP)]
    )
    context_grad = jnp.concatenate(
        [quad[:, :, :width], to_peer(quad[:, :, width:], CORE_HOP)], axis=0
    ).reshape(rows, width)
    attn_grad_all = gather_plane(attn_grad).reshape(rows, feat)

    qkv_grad = attend_back(rank_arg, slopes, qkv, context_grad, tops)
    qkv_grad_weight = dot_tn(normed_low, qkv_grad)
    qkv_owned = ring_scatter(qkv_grad_weight, 0)
    out_grad_weight = dot_tn(context, attn_grad_all)
    out_owned = ring_scatter(out_grad_weight, 1)
    norm_one_grad = scatter_plane(qkv_grad, qkv_low, ((1,), (1,)))
    downward = scatter_plane(activated, down_low, ((1,), (0,)))
    layer_out = turn_blocks((hidden_rows + downward + bias_down).astype(low), 1)

    own_f = tok_own.astype(f32)
    own_mean, own_scale = norm_stats(own_f)
    own_hat = (own_f - own_mean) * own_scale
    token_grad = turn_blocks(
        hidden_grad + norm_back(norm_one_grad, own_hat, own_scale, gain_one), 1
    )

    one = (rank == 0).astype(f32)
    wide_terms = turn_blocks(
        jnp.stack(
            [
                jnp.sum(norm_one_grad * own_hat, axis=0),
                jnp.sum(norm_one_grad, axis=0),
                jnp.sum(attn_grad.astype(f32), axis=0),
                jnp.sum(norm_two_grad * hat_two, axis=0),
                jnp.sum(norm_two_grad, axis=0),
                jnp.sum(out_grad.astype(f32), axis=0),
            ]
        ),
        1,
    )
    sums = jnp.sum(qkv_grad.astype(f32), axis=0)
    zero = jnp.zeros((feat,), f32)
    query_slot = lax.dynamic_update_slice(zero, sums[:width], (head_at,))
    value_slot = lax.dynamic_update_slice(zero, sums[2 * width :], (head_at,))
    up_slot = lax.dynamic_update_slice(
        jnp.zeros((8 * hidden,), f32), jnp.sum(up_grad.astype(f32), axis=0), (hidden_at,)
    )
    vector_grad = scatter_vectors(
        jnp.concatenate(
            [
                wide_terms[0],
                wide_terms[1],
                query_slot,
                value_slot,
                wide_terms[2],
                wide_terms[3],
                wide_terms[4],
                wide_terms[5],
                up_slot,
            ]
        )
    )

    def owned(total, column_axis, feature_axis):
        keep, send = pick_half(first, total, feature_axis)
        return in_order(first, keep, swap_ctx(send.astype(low)).astype(f32), column_axis)

    keep, send = pick_half(first, qkv_owned, 0)
    got = swap_ctx(send.astype(low)).astype(f32)
    qkv_final = jnp.stack(
        [
            in_order(
                first, keep[:, i * width : (i + 1) * width], got[:, i * width : (i + 1) * width], 1
            )
            for i in range(3)
        ]
    )
    out_final = owned(out_owned, 0, 1)
    up_final = owned(up_owned, 1, 0)
    down_final = owned(down_owned, 0, 1)

    qkv_moment, qkv_square, qkv_new = adam_update(
        qkv_weight, qkv_final, qkv_first, qkv_second, rate_matrix, decay_coef
    )
    out_moment, out_square, out_new = adam_update(
        out_weight, out_final, out_first, out_second, rate_matrix, decay_coef
    )
    up_moment, up_square, up_new = adam_update(
        up_weight, up_final, up_first, up_second, rate_matrix, decay_coef
    )
    down_moment, down_square, down_new = adam_update(
        down_weight, down_final, down_first, down_second, rate_matrix, decay_coef
    )
    vec_moment, vec_square, vec_new = adam_update(
        vectors, vector_grad, vec_first, vec_second, rate_vector, 0.0
    )
    return (
        layer_out,
        token_grad,
        qkv_moment,
        out_moment,
        up_moment,
        down_moment,
        vec_moment,
        qkv_square,
        out_square,
        up_square,
        down_square,
        vec_square,
        qkv_new,
        out_new,
        up_new,
        down_new,
        vec_new,
    )


def solution(mesh):
    rows = P(("shard", "ctx"), None)
    shares = P(ALL, None)
    weights = (
        P(None, ("shard", "ctx"), "tensor"),
        P("tensor", ("shard", "ctx")),
        P(("shard", "ctx"), "tensor"),
        P("tensor", ("shard", "ctx")),
        P(ALL),
    )
    return jax.shard_map(
        per_device,
        mesh=mesh,
        in_specs=(rows, rows, P("shard")) + weights * 3,
        out_specs=(shares, shares) + weights * 3,
        check_vma=False,
    )
```

```python
import functools

import jax
import jax.numpy as jnp
from jax import lax
from jax.experimental import pallas as pl
from jax.experimental.pallas import tpu as pltpu
from jax.sharding import PartitionSpec as P

HEADS = 16
HDIM = 64
STEP = 10
ALL = ("shard", "ctx", "tensor")
PLANE = ("ctx", "tensor")

norm_eps = 1e-05
mask_value = -1e30
beta_first = 0.9
beta_second = 0.95
adam_eps = 1e-08
decay_coef = 0.1
rate_matrix = 0.05
rate_vector = 0.6

low = jnp.bfloat16
f32 = jnp.float32


def mask_of(j):
    return ((j & 3) << 1) | (j >> 2)


def rel_of(mask):
    return ((mask & 1) << 2) | (mask >> 1)


def to_peer(value, mask):
    return lax.ppermute(value, PLANE, [(i, i ^ mask) for i in range(8)])


X_HOP, Y_HOP, XY_HOP, CORE_HOP = 4, 2, 6, 1


def along_shard(value, steps):
    count = lax.axis_size("shard")
    return lax.ppermute(value, "shard", [(i, (i + steps) % count) for i in range(count)])


def swap_ctx(value):
    return lax.ppermute(value, "ctx", [(0, 1), (1, 0)])


def in_order(first, own, other, axis):
    return jnp.where(
        first, jnp.concatenate([own, other], axis), jnp.concatenate([other, own], axis)
    )


def pick_half(first, value, axis):
    a, b = jnp.split(value, 2, axis=axis)
    return jnp.where(first, a, b), jnp.where(first, b, a)


def adam_update(weight, gradient, first_mom, second, step_rate, decay_here):
    moment = beta_first * first_mom + (1.0 - beta_first) * gradient
    square = beta_second * second + (1.0 - beta_second) * gradient * gradient
    ratio = (
        moment
        / (1.0 - beta_first**STEP)
        / (jnp.sqrt(square / (1.0 - beta_second**STEP)) + adam_eps)
    )
    new_weight = weight - step_rate * (ratio + decay_here * weight)
    return (moment, square, new_weight)


def norm_stats(values):
    row_mean = jnp.mean(values, axis=-1, keepdims=True)
    centred = values - row_mean
    row_var = jnp.mean(centred * centred, axis=-1, keepdims=True)
    return row_mean, lax.rsqrt(row_var + norm_eps)


def norm_back(grad, hat, scale, gain):
    scaled = grad * gain
    inner = jnp.mean(scaled * hat, axis=-1, keepdims=True)
    return scale * (scaled - jnp.mean(scaled, axis=-1, keepdims=True) - hat * inner)


BLOCK = 256


def dot_nt(a, b):
    return lax.dot_general(a, b, (((1,), (1,)), ((), ())), preferred_element_type=f32)


def dot_nn(a, b):
    return lax.dot_general(a, b, (((1,), (0,)), ((), ())), preferred_element_type=f32)


def dot_tn(a, b):
    return lax.dot_general(a, b, (((0,), (0,)), ((), ())), preferred_element_type=f32)


def block_of(rank, b):
    return pl.multiple_of(rel_of(b ^ rank) * 128, 128)


def score_pieces(nat, slope, head, at):
    lanes = pl.ds(head * HDIM, HDIM)
    query = nat[pl.ds(at * BLOCK, BLOCK), lanes] * low(HDIM**-0.5)
    pieces = []
    spans = ([(0, at * BLOCK)] if at else []) + [(at * BLOCK, BLOCK)]
    for start, size in spans:
        key = nat[pl.ds(start, size), pl.ds(128 + head * HDIM, HDIM)]
        raw = dot_nt(key, query)
        down = lax.broadcasted_iota(jnp.int32, (size, BLOCK), 0)
        raw = raw + slope * (down + (start - at * BLOCK)).astype(f32)
        if start == at * BLOCK:
            across = lax.broadcasted_iota(jnp.int32, (size, BLOCK), 1)
            raw = jnp.where(down <= across, raw, mask_value)
        pieces.append((start, size, key, raw))
    return query, pieces


smem = pl.BlockSpec(memory_space=pltpu.SMEM)
vmem = pl.BlockSpec(memory_space=pltpu.VMEM)


def shape(dims, dtype):
    return jax.ShapeDtypeStruct(dims, dtype)


def run(body, outs, args, scratch=(), flops=0):
    moved = sum(a.size * a.dtype.itemsize for a in args) + sum(
        o.size * jnp.dtype(o.dtype).itemsize for o in outs
    )
    return pl.pallas_call(
        body,
        out_shape=tuple(outs),
        in_specs=[smem if a.ndim == 1 else vmem for a in args],
        out_specs=tuple(vmem for _ in outs),
        scratch_shapes=list(scratch),
        compiler_params=pltpu.CompilerParams(vmem_limit_bytes=40 * 1024 * 1024),
        cost_estimate=pl.CostEstimate(flops=flops, bytes_accessed=moved, transcendentals=0),
    )(*args)


RANK, CTX, ROW_Y, CORE, LIVE, BLOCKS = 0, 1, 2, 3, 4, 5


def feature_at(ints, k):
    return pl.multiple_of(ints[BLOCKS + k] * 256, 256)


def rows_of(ints, local, got, swapped, j):
    dc, dx, dy = j >> 2, (j >> 1) & 1, j & 1
    y, c = ints[ROW_Y] ^ dy, ints[CORE] ^ dc
    if dx == 0:
        return local[pl.ds(pl.multiple_of((y * 2 + c) * 128, 128), 128), :]
    there = pl.ds(pl.multiple_of(y * 128, 128), 128)
    return (swapped if dc else got)[there, :]


def pack_kernel(ints, qkv, out, up, down, own_a, send_a, own_b, send_b):
    ctx = ints[CTX]
    for mine, a, b in ((True, own_a, own_b), (False, send_a, send_b)):
        half = ctx if mine else 1 - ctx
        at = pl.ds(pl.multiple_of(half * 128, 128), 128)
        for i in range(3):
            a[:, pl.ds(i * 128, 128)] = qkv[i, :, at].astype(low)
        a[:, pl.ds(384, 128)] = out[at, :].astype(low)
        b[pl.ds(0, 128), :] = up[:, pl.ds(pl.multiple_of(half * 512, 512), 512)].astype(low)
        for i in range(4):
            tile = pl.ds(pl.multiple_of(half * 512 + i * 128, 128), 128)
            b[pl.ds(128, 128), pl.ds(i * 128, 128)] = down[tile, :].astype(low)


def norm_kernel(ints, vec, local, got, swapped, out):
    for j in range(8):
        values = rows_of(ints, local, got, swapped, j).astype(f32)
        mean, scale = norm_stats(values)
        out[pl.ds(j * 128, 128), :] = (
            (values - mean) * scale * vec[pl.ds(0, 1), :] + vec[pl.ds(1, 1), :]
        ).astype(low)


def mask_kernel(ints, local, got, swapped, out):
    for j in range(8):
        values = rows_of(ints, local, got, swapped, j)
        start = (ints[RANK] ^ mask_of(j)) * 128
        place = start + lax.broadcasted_iota(jnp.int32, values.shape, 0)
        out[pl.ds(j * 128, 128), :] = jnp.where(
            place < ints[LIVE], values.astype(f32), 0.0
        ).astype(low)


def out_kernel(ints, a0, a1, a2, a3, out):
    for k, a in enumerate((a0, a1, a2, a3)):
        for x in range(2):
            at = pl.multiple_of(ints[BLOCKS + k] * 256 + x * 128, 128)
            out[:, pl.ds(at, 128)] = a[pl.ds(x * 128, 128), pl.ds(384, 128)]


def attend_kernel(ints, slope_ref, vec, normed, a0, a1, a2, a3, qkv_ref, out_ref, top_ref, nat):
    rank, ctx = ints[RANK], ints[CTX]
    rows = normed.shape[0]
    part = rank - ctx * 4
    head_at = pl.ds(pl.multiple_of(part * 256 + ctx * 128, 128), 128)
    total = jnp.zeros((rows, 384), f32)
    for k, a in enumerate((a0, a1, a2, a3)):
        total = total + dot_nn(normed[:, pl.ds(feature_at(ints, k), 256)], a[:, pl.ds(0, 384)])
    for i, row in ((0, 2), (1, None), (2, 3)):
        some = total[:, i * 128 : (i + 1) * 128]
        if row is not None:
            some = some + vec[pl.ds(row, 1), head_at]
        qkv_ref[:, pl.ds(i * 128, 128)] = some.astype(low)
    for b in range(rows // 128):
        nat[pl.ds(b * 128, 128), :] = qkv_ref[pl.ds(block_of(rank, b), 128), :]
    for at in range(rows // BLOCK):
        outs = []
        for head in range(2):
            _, pieces = score_pieces(nat, slope_ref[head], head, at)
            top = functools.reduce(
                jnp.maximum, [jnp.max(raw, axis=0, keepdims=True) for _, _, _, raw in pieces]
            )
            probs = [jnp.exp(raw - top) for _, _, _, raw in pieces]
            total = sum(jnp.sum(p, axis=0, keepdims=True) for p in probs)
            inverse = 1.0 / total
            mixed = jnp.zeros((HDIM, BLOCK), f32)
            for (start, size, _, _), p in zip(pieces, probs):
                value = nat[pl.ds(start, size), pl.ds(256 + head * HDIM, HDIM)]
                mixed = mixed + dot_tn(value, (p * inverse).astype(low))
            outs.append(mixed.T)
            top_ref[pl.ds(head, 1), pl.ds(at * BLOCK, BLOCK)] = top + jnp.log(total)
        both = jnp.concatenate(outs, axis=1).astype(low)
        for part in range(BLOCK // 128):
            b = at * (BLOCK // 128) + part
            out_ref[pl.ds(block_of(rank, b), 128), :] = both[part * 128 : (part + 1) * 128]


def hidden_kernel(ints, vec, local, q0, q1, q2, q3, *refs):
    outs, (hidden, hat, scale_out, normed) = refs[:8], refs[8:]
    part = ints[RANK] - ints[CTX] * 4
    total = local[pl.ds(pl.multiple_of(part * 128, 128), 128), :].astype(f32)
    total = total + vec[pl.ds(4, 1), :]
    for c in range(2):
        for i, q in enumerate((q0, q1, q2, q3)):
            total = total + dot_nn(q[:, pl.ds(c * 128, 128)], outs[c * 4 + i][...])
    mean, scale = norm_stats(total)
    centred = (total - mean) * scale
    hidden[...] = total
    hat[...] = centred
    scale_out[...] = jnp.broadcast_to(scale, scale_out.shape)
    normed[...] = (centred * vec[pl.ds(5, 1), :] + vec[pl.ds(6, 1), :]).astype(low)


def unpack_up(ints, blocks, up):
    for k, b in enumerate(blocks):
        for x in range(2):
            at = pl.ds(pl.multiple_of(ints[BLOCKS + k] * 256 + x * 128, 128), 128)
            up[at, :] = b[pl.ds(x * 256, 128), :]


def unpack_down(ints, blocks, down):
    for k, b in enumerate(blocks):
        for x in range(2):
            at = pl.ds(pl.multiple_of(ints[BLOCKS + k] * 256 + x * 128, 128), 128)
            for i in range(4):
                down[pl.ds(i * 128, 128), at] = b[pl.ds(x * 256 + 128, 128), pl.ds(i * 128, 128)]


def forward_back_kernel(ints, vec, grad, *refs):
    normed, blocks = refs[:8], refs[8:12]
    act, up_grad, far, near, sums, whole, up, down = refs[12:]
    for j in range(8):
        whole[pl.ds(j * 128, 128), :] = normed[j][...]
    unpack_up(ints, blocks, up)
    unpack_down(ints, blocks, down)
    part = ints[RANK] - ints[CTX] * 4
    bias = vec[pl.ds(8 + part, 1), pl.ds(pl.multiple_of(ints[CTX] * 512, 512), 512)]
    coef = 0.7978845608028654
    bias_sum = jnp.zeros((1, 512), f32)
    for half in (1, 0):
        at = pl.ds(half * 512, 512)
        upward = dot_nn(whole[at, :], up[...]) + bias
        act_grad = dot_nt(grad[at, :], down[...])
        square = upward * upward
        tanh = jnp.tanh(coef * (upward + 0.044715 * square * upward))
        act[at, :] = (0.5 * upward * (1.0 + tanh)).astype(low)
        slope = 0.5 * (1.0 + tanh) + 0.5 * upward * (1.0 - tanh * tanh) * coef * (
            1.0 + 3.0 * 0.044715 * square
        )
        pre = (act_grad * slope).astype(low)
        up_grad[at, :] = pre
        bias_sum = bias_sum + jnp.sum(pre.astype(f32), axis=0, keepdims=True)
        back = dot_nt(pre, up[...])
        if half:
            far[...] = back.astype(low)
        else:
            near[...] = back
    sums[...] = bias_sum


def weight_grad_kernel(ints, grad, act, up_grad, *refs):
    normed, blocks = refs[:8], refs[8:12]
    g0, g1, g2, g3, far, near, whole, down = refs[12:]
    for j in range(8):
        whole[pl.ds(j * 128, 128), :] = normed[j][...]
    unpack_down(ints, blocks, down)
    for k, g in reversed(tuple(enumerate((g0, g1, g2, g3)))):
        at = pl.ds(feature_at(ints, k), 256)
        ups = dot_tn(whole[:, at], up_grad[...]).astype(low)
        downs = dot_tn(act[...], grad[:, at]).astype(low)
        for x in range(2):
            g[pl.ds(x * 256, 128), :] = ups[x * 128 : (x + 1) * 128]
            for i in range(4):
                g[pl.ds(x * 256 + 128, 128), pl.ds(i * 128, 128)] = downs[
                    i * 128 : (i + 1) * 128, x * 128 : (x + 1) * 128
                ]
    far[...] = dot_nn(act[pl.ds(512, 512), :], down[...]).astype(low)
    near[...] = dot_nn(act[pl.ds(0, 512), :], down[...])


def hidden_back_kernel(ints, vec, own, p0, p1, p2, hat, scale, grad, *refs):
    outs, (hidden_grad, attn_grad, pairs, sums) = refs[:8], refs[8:]
    total = own[...] + p0[...].astype(f32) + p1[...].astype(f32) + p2[...].astype(f32)
    hats = hat[...]
    live = grad[pl.ds(0, 128), :].astype(f32)
    back = live + norm_back(total, hats, scale[:, pl.ds(0, 1)], vec[pl.ds(5, 1), :])
    hidden_grad[...] = back
    rounded = back.astype(low)
    attn_grad[...] = rounded
    for c in range(2):
        for i in range(4):
            pairs[i, :, pl.ds(c * 128, 128)] = dot_nt(rounded, outs[c * 4 + i][...]).astype(low)
    for i, value in enumerate((rounded.astype(f32), total * hats, total, live)):
        sums[pl.ds(i, 1), :] = jnp.sum(value, axis=0, keepdims=True)


def attend_back_kernel(ints, slope_ref, normed, qkv_ref, top_ref, context, swapped, *refs):
    pieces_in, fulls, weights = refs[:4], refs[4:12], refs[12:16]
    g0, g1, g2, g3, far, near, sums, nat, gnat, acc, rel, full = refs[16:]
    rank = ints[RANK]
    rows = qkv_ref.shape[0]
    for i in range(4):
        gnat[pl.ds(pl.multiple_of((rank ^ mask_of(i)) * 128, 128), 128), :] = pieces_in[i][
            :, pl.ds(0, 128)
        ]
        there = pl.multiple_of((rank ^ mask_of(4 + i)) * 128, 128)
        gnat[pl.ds(there, 128), :] = swapped[pl.ds(i * 128, 128), :]
    for b in range(rows // 128):
        nat[pl.ds(b * 128, 128), :] = qkv_ref[pl.ds(block_of(rank, b), 128), :]
        full[pl.ds(b * 128, 128), :] = fulls[b][...]
    for head in range(2):
        for at in range(rows // BLOCK - 1, -1, -1):
            here = pl.ds(at * BLOCK, BLOCK)
            query, pieces = score_pieces(nat, slope_ref[head], head, at)
            grad = gnat[here, pl.ds(head * HDIM, HDIM)]
            log_total = top_ref[pl.ds(head, 1), here]
            probs, slopes = [], []
            inner = jnp.zeros((1, BLOCK), f32)
            for start, size, _, raw in pieces:
                value = nat[pl.ds(start, size), pl.ds(256 + head * HDIM, HDIM)]
                p = jnp.exp(raw - log_total)
                d = dot_nt(value, grad)
                inner = inner + jnp.sum(p * d, axis=0, keepdims=True)
                probs.append(p)
                slopes.append(d)
            query_grad = jnp.zeros((HDIM, BLOCK), f32)
            for (start, size, key, _), p, d in zip(pieces, probs, slopes):
                s = (p * (d - inner)).astype(low)
                query_grad = query_grad + dot_tn(key, s)
                key_grad = dot_nn(s, query)
                value_grad = dot_nn(p.astype(low), grad)
                k_at = (pl.ds(start, size), pl.ds(128 + head * HDIM, HDIM))
                v_at = (pl.ds(start, size), pl.ds(256 + head * HDIM, HDIM))
                if at == rows // BLOCK - 1:
                    acc[k_at] = key_grad
                    acc[v_at] = value_grad
                else:
                    acc[k_at] += key_grad
                    acc[v_at] += value_grad
            acc[here, pl.ds(head * HDIM, HDIM)] = query_grad.T * (HDIM**-0.5)
    bias_sum = jnp.zeros((1, 384), f32)
    for b in range(rows // 128):
        some = acc[pl.ds(b * 128, 128), :].astype(low)
        bias_sum = bias_sum + jnp.sum(some.astype(f32), axis=0, keepdims=True)
        rel[pl.ds(block_of(rank, b), 128), :] = some
    sums[...] = bias_sum
    for k in range(3, -1, -1):
        g, w = (g0, g1, g2, g3)[k], weights[k]
        at = pl.ds(feature_at(ints, k), 256)
        g[:, pl.ds(0, 384)] = dot_tn(normed[:, at], rel[...]).astype(low)
        outs = dot_tn(context[...], full[:, at]).astype(low)
        for x in range(2):
            g[pl.ds(x * 128, 128), pl.ds(384, 128)] = outs[:, x * 128 : (x + 1) * 128]
        far[:, at] = dot_nt(rel[pl.ds(512, 512), :], w[:, pl.ds(0, 384)]).astype(low)
        near[:, at] = dot_nt(rel[pl.ds(0, 512), :], w[:, pl.ds(0, 384)])


def last_kernel(ints, vec, local, own, p0, p1, p2, hidden_grad, wide, qkv_sums, up_sums, out, term):
    ctx = ints[CTX]
    part = ints[RANK] - ctx * 4
    values = local[pl.ds(pl.multiple_of(part * 128, 128), 128), :].astype(f32)
    mean, scale = norm_stats(values)
    hat = (values - mean) * scale
    total = own[...] + p0[...].astype(f32) + p1[...].astype(f32) + p2[...].astype(f32)
    out[...] = hidden_grad[...] + norm_back(total, hat, scale, vec[pl.ds(0, 1), :])
    term[...] = jnp.zeros_like(term)
    term[pl.ds(0, 1), :] = jnp.sum(total * hat, axis=0, keepdims=True)
    term[pl.ds(1, 1), :] = jnp.sum(total, axis=0, keepdims=True)
    head_at = pl.ds(pl.multiple_of(part * 256 + ctx * 128, 128), 128)
    term[pl.ds(2, 1), head_at] = qkv_sums[:, pl.ds(0, 128)]
    term[pl.ds(3, 1), head_at] = qkv_sums[:, pl.ds(256, 128)]
    term[pl.ds(4, 4), :] = wide[...]
    term[pl.ds(8 + part, 1), pl.ds(pl.multiple_of(ctx * 512, 512), 512)] = up_sums[...]


def adam_attn_kernel(ints, keep, got, qw, qf, qs, ow, of, os, qm, qq, qn, om, oq, on):
    ctx = ints[CTX]
    for source, half in ((keep, ctx), (got, 1 - ctx)):
        at = pl.ds(pl.multiple_of(half * 128, 128), 128)
        for i in range(3):
            g = source[:, pl.ds(i * 128, 128)].astype(f32)
            qm[i, :, at], qq[i, :, at], qn[i, :, at] = adam_update(
                qw[i, :, at], g, qf[i, :, at], qs[i, :, at], rate_matrix, decay_coef
            )
        g = source[:, pl.ds(384, 128)].astype(f32)
        om[at, :], oq[at, :], on[at, :] = adam_update(
            ow[at, :], g, of[at, :], os[at, :], rate_matrix, decay_coef
        )


def adam_ff_kernel(ints, keep, got, uw, uf, us, dw, df, ds, um, uq, un, dm, dq, dn):
    ctx = ints[CTX]
    for source, half in ((keep, ctx), (got, 1 - ctx)):
        at = pl.ds(pl.multiple_of(half * 512, 512), 512)
        g = source[pl.ds(0, 128), :].astype(f32)
        um[:, at], uq[:, at], un[:, at] = adam_update(
            uw[:, at], g, uf[:, at], us[:, at], rate_matrix, decay_coef
        )
        for i in range(4):
            tile = pl.ds(pl.multiple_of(half * 512 + i * 128, 128), 128)
            g = source[pl.ds(128, 128), pl.ds(i * 128, 128)].astype(f32)
            dm[tile, :], dq[tile, :], dn[tile, :] = adam_update(
                dw[tile, :], g, df[tile, :], ds[tile, :], rate_matrix, decay_coef
            )


def gather_blocks(block):
    quad = [block, to_peer(block, Y_HOP), to_peer(block, X_HOP), to_peer(block, XY_HOP)]
    return quad + [to_peer(one, CORE_HOP) for one in quad]


def scatter_halves(far, near):
    got = to_peer(far, CORE_HOP)
    quad = (near + got.astype(f32)).reshape(4, 128, -1)
    parts = quad[1:].astype(low)
    return (
        quad[0],
        to_peer(parts[0], Y_HOP),
        to_peer(parts[1], X_HOP),
        to_peer(parts[2], XY_HOP),
    )


def ring_blocks(block):
    blocks = [block]
    for _ in range(3):
        blocks.append(along_shard(blocks[-1], 1))
    return blocks


def ring_sum(blocks):
    total = blocks[3]
    for k in (2, 1, 0):
        total = along_shard(total, -1).astype(f32) + blocks[k].astype(f32)
        if k:
            total = total.astype(low)
    return total


def pack_attn(qkv, out):
    return [
        jnp.concatenate(
            [
                qkv[k * 256 : (k + 1) * 256],
                jnp.concatenate(jnp.split(out[:, k * 256 : (k + 1) * 256], 2, axis=1), axis=0),
            ],
            axis=1,
        )
        for k in range(4)
    ]


def unpack_attn(blocks):
    qkv = jnp.concatenate([b[:, :384] for b in blocks], axis=0)
    out = jnp.concatenate(
        [b[x * 128 : (x + 1) * 128, 384:] for b in blocks for x in range(2)], axis=1
    )
    return qkv, out


def pack_ff(up, down):
    blocks = []
    for k in range(4):
        parts = []
        for x in range(2):
            at = k * 256 + x * 128
            parts.append(up[at : at + 128])
            parts.append(
                jnp.concatenate(jnp.split(down[:, at : at + 128], 4, axis=0), axis=1)
            )
        blocks.append(jnp.concatenate(parts, axis=0))
    return blocks


def unpack_ff(blocks):
    ups, downs = [], []
    for b in blocks:
        for x in range(2):
            ups.append(b[x * 256 : x * 256 + 128])
            tiles = b[x * 256 + 128 : x * 256 + 256]
            downs.append(jnp.concatenate(jnp.split(tiles, 4, axis=1), axis=0))
    return jnp.concatenate(ups, axis=0), jnp.concatenate(downs, axis=1)


def per_device(
    tokens,
    cotangent,
    lengths,
    qkv_weight,
    out_weight,
    up_weight,
    down_weight,
    vectors,
    qkv_first,
    out_first,
    up_first,
    down_first,
    vec_first,
    qkv_second,
    out_second,
    up_second,
    down_second,
    vec_second,
):
    tok_rows, feat = tokens.shape
    shards = lax.axis_size("shard")
    ringed = feat // shards == 256
    ctx = lax.axis_index("ctx")
    part = lax.axis_index("tensor")
    place = lax.axis_index("shard")
    first = ctx == 0
    rank = ctx * 4 + part
    rows = 2 * tok_rows
    order = [lax.rem(place - k + shards, shards) if ringed else k for k in range(4)]
    ints = jnp.stack(
        [jnp.asarray(i, jnp.int32) for i in [rank, ctx, part // 2, part % 2, lengths[0]] + order]
    )

    if ringed:
        own_a, send_a, own_b, send_b = run(
            pack_kernel,
            [shape((128, 512), low)] * 2 + [shape((256, 512), low)] * 2,
            [ints, qkv_weight, out_weight, up_weight, down_weight],
        )
        block_a = in_order(first, own_a, swap_ctx(send_a), 0)
        attn_weights = ring_blocks(block_a)
    else:

        def fetch(weight, column_axis, feature_axis):
            own, send = pick_half(first, weight.astype(low), column_axis)
            whole = in_order(first, own, swap_ctx(send), feature_axis)
            return lax.all_gather(whole, "shard", axis=feature_axis, tiled=True)

        qkv_flat = jnp.concatenate(
            [qkv_weight[i][:, h * 128 : (h + 1) * 128] for h in range(2) for i in range(3)], axis=1
        )
        attn_weights = pack_attn(fetch(qkv_flat, 1, 0), fetch(out_weight, 0, 1))

    def other_rows(value):
        mine = value.reshape(2, 2, 128, feat)
        got = swap_ctx(
            lax.dynamic_index_in_dim(mine, part % 2, 1, keepdims=False).reshape(256, feat)
        )
        return got, to_peer(got, CORE_HOP)

    got, swapped = other_rows(tokens)
    every = lax.all_to_all(
        jnp.broadcast_to(vectors[None], (8 * shards,) + vectors.shape), ALL, 0, 0, tiled=True
    )
    vec = every.reshape(12, feat)
    normed_one = run(
        norm_kernel, [shape((rows, feat), low)], [ints, vec, tokens, got, swapped]
    )[0]

    if ringed:
        block_b = in_order(first, own_b, swap_ctx(send_b), 0)
        ff_weights = ring_blocks(block_b)
    else:
        ff_weights = pack_ff(fetch(up_weight, 1, 0), fetch(down_weight, 0, 1))

    out_local = run(out_kernel, [shape((128, feat), low)], [ints] + attn_weights)[0]
    out_blocks = gather_blocks(out_local)

    slopes_all = jnp.exp2(-8.0 * (jnp.arange(HEADS).astype(f32) + 1.0) / HEADS)
    slopes = lax.dynamic_slice_in_dim(slopes_all, part * 4 + ctx * 2, 2)
    qkv, context, tops = run(
        attend_kernel,
        [shape((rows, 384), low), shape((rows, 128), low), shape((8, rows), f32)],
        [ints, slopes, vec, normed_one] + attn_weights,
        [pltpu.VMEM((rows, 384), low)],
        flops=2 * rows * feat * 384 + 6 * rows * rows * HDIM,
    )

    cot_got, cot_swapped = other_rows(cotangent)
    out_grad = run(
        mask_kernel, [shape((rows, feat), low)], [ints, cotangent, cot_got, cot_swapped]
    )[0]

    blocks = context.reshape(2, 4, 128, 128)
    quad = jnp.concatenate([blocks[0], to_peer(blocks[1], CORE_HOP)], axis=2)
    quad = [quad[0], to_peer(quad[1], Y_HOP), to_peer(quad[2], X_HOP), to_peer(quad[3], XY_HOP)]
    hidden_rows, hat_two, scale_two, normed_own = run(
        hidden_kernel,
        [shape((128, feat), f32), shape((128, feat), f32), shape((128, 128), f32)]
        + [shape((128, feat), low)],
        [ints, vec, tokens] + quad + out_blocks,
        flops=2 * 128 * feat * feat,
    )
    normed_two = gather_blocks(normed_own)

    activated, up_grad, far, near, up_sums = run(
        forward_back_kernel,
        [shape((rows, 512), low)] * 2
        + [shape((512, feat), low), shape((512, feat), f32), shape((1, 512), f32)],
        [ints, vec, out_grad] + normed_two + ff_weights,
        [pltpu.VMEM((rows, feat), low), pltpu.VMEM((feat, 512), low), pltpu.VMEM((512, feat), low)],
        flops=6 * rows * feat * 512,
    )
    norm_two_parts = scatter_halves(far, near)
    *ff_grads, down_far, down_near = run(
        weight_grad_kernel,
        [shape((512, 512), low)] * 4 + [shape((512, feat), low), shape((512, feat), f32)],
        [ints, out_grad, activated, up_grad] + normed_two + ff_weights,
        [pltpu.VMEM((rows, feat), low), pltpu.VMEM((512, feat), low)],
        flops=6 * rows * feat * 512,
    )
    hidden_grad, attn_grad, pairs, wide = run(
        hidden_back_kernel,
        [shape((128, feat), f32), shape((128, feat), low)]
        + [shape((4, 128, 256), low), shape((4, feat), f32)],
        [ints, vec, *norm_two_parts, hat_two, scale_two, out_grad] + out_blocks,
        flops=2 * 128 * feat * feat,
    )
    quad = [pairs[0], to_peer(pairs[1], Y_HOP), to_peer(pairs[2], X_HOP), to_peer(pairs[3], XY_HOP)]
    crossing = to_peer(jnp.concatenate([q[:, 128:] for q in quad], axis=0), CORE_HOP)
    attn_grads = gather_blocks(attn_grad)
    *grads, far, near, qkv_sums = run(
        attend_back_kernel,
        [shape((256, 512), low)] * 4
        + [shape((512, feat), low), shape((512, feat), f32), shape((1, 384), f32)],
        [ints, slopes, normed_one, qkv, tops, context, crossing]
        + quad
        + attn_grads
        + attn_weights,
        [
            pltpu.VMEM((rows, 384), low),
            pltpu.VMEM((rows, 128), low),
            pltpu.VMEM((rows, 384), f32),
            pltpu.VMEM((rows, 384), low),
            pltpu.VMEM((rows, feat), low),
        ],
        flops=15 * rows * rows * HDIM + 4 * rows * feat * 384 + 2 * rows * feat * 128,
    )
    norm_one_parts = scatter_halves(far, near)
    down_parts = scatter_halves(down_far, down_near)
    layer_out = (
        hidden_rows + vec[7:8] + sum(p.astype(f32) for p in down_parts)
    ).astype(low)

    token_grad, term = run(
        last_kernel,
        [shape((128, feat), f32), shape((12, feat), f32)],
        [ints, vec, tokens, *norm_one_parts, hidden_grad, wide, qkv_sums, up_sums],
    )
    vector_grad = jnp.sum(
        lax.all_to_all(term.reshape((8 * shards,) + vectors.shape), ALL, 0, 0, tiled=True), axis=0
    )

    def settle(total):
        keep, send = pick_half(first, total, 0)
        return keep, swap_ctx(send.astype(low))

    if ringed:
        keep_b, got_b = settle(ring_sum(ff_grads))
        keep_a, got_a = settle(ring_sum(grads))
    else:

        def owned(total, column_axis, feature_axis):
            total = lax.psum_scatter(
                total.astype(f32), "shard", scatter_dimension=feature_axis, tiled=True
            )
            keep, send = pick_half(first, total, feature_axis)
            return in_order(first, keep, swap_ctx(send.astype(low)).astype(f32), column_axis)

        qkv_total, out_total = unpack_attn(grads)
        up_total, down_total = unpack_ff(ff_grads)
        qkv_total = jnp.split(qkv_total, 3, axis=1)
        qkv_owned = jnp.stack([owned(g, 1, 0) for g in qkv_total])
        out_owned = owned(out_total, 0, 1)
        up_owned = owned(up_total, 1, 0)
        down_owned = owned(down_total, 0, 1)

    if ringed:
        up_moment, up_square, up_new, down_moment, down_square, down_new = run(
            adam_ff_kernel,
            [shape(up_weight.shape, f32)] * 3 + [shape(down_weight.shape, f32)] * 3,
            [ints, keep_b, got_b, up_weight, up_first, up_second]
            + [down_weight, down_first, down_second],
        )
        qkv_moment, qkv_square, qkv_new, out_moment, out_square, out_new = run(
            adam_attn_kernel,
            [shape(qkv_weight.shape, f32)] * 3 + [shape(out_weight.shape, f32)] * 3,
            [ints, keep_a, got_a, qkv_weight, qkv_first, qkv_second]
            + [out_weight, out_first, out_second],
        )
    else:
        qkv_moment, qkv_square, qkv_new = adam_update(
            qkv_weight, qkv_owned, qkv_first, qkv_second, rate_matrix, decay_coef
        )
        out_moment, out_square, out_new = adam_update(
            out_weight, out_owned, out_first, out_second, rate_matrix, decay_coef
        )
        up_moment, up_square, up_new = adam_update(
            up_weight, up_owned, up_first, up_second, rate_matrix, decay_coef
        )
        down_moment, down_square, down_new = adam_update(
            down_weight, down_owned, down_first, down_second, rate_matrix, decay_coef
        )
    vec_moment, vec_square, vec_new = adam_update(
        vectors, vector_grad, vec_first, vec_second, rate_vector, 0.0
    )
    return (
        layer_out,
        token_grad,
        qkv_moment,
        out_moment,
        up_moment,
        down_moment,
        vec_moment,
        qkv_square,
        out_square,
        up_square,
        down_square,
        vec_square,
        qkv_new,
        out_new,
        up_new,
        down_new,
        vec_new,
    )


def solution(mesh):
    rows = P(("shard", "ctx"), None)
    shares = P(ALL, None)
    weights = (
        P(None, ("shard", "ctx"), "tensor"),
        P("tensor", ("shard", "ctx")),
        P(("shard", "ctx"), "tensor"),
        P("tensor", ("shard", "ctx")),
        P(ALL),
    )
    return jax.shard_map(
        per_device,
        mesh=mesh,
        in_specs=(rows, rows, P("shard")) + weights * 3,
        out_specs=(shares, shares) + weights * 3,
        check_vma=False,
    )
```

```python
import functools

import jax
import jax.numpy as jnp
from jax import lax
from jax.experimental import pallas as pl
from jax.experimental.pallas import tpu as pltpu
from jax.sharding import PartitionSpec as P

HEADS = 16
HDIM = 64
STEP = 10
ALL = ("shard", "ctx", "tensor")
PLANE = ("ctx", "tensor")

norm_eps = 1e-05
mask_value = -1e30
beta_first = 0.9
beta_second = 0.95
adam_eps = 1e-08
decay_coef = 0.1
rate_matrix = 0.05
rate_vector = 0.6

low = jnp.bfloat16
f32 = jnp.float32


def mask_of(j):
    return ((j & 3) << 1) | (j >> 2)


def rel_of(mask):
    return ((mask & 1) << 2) | (mask >> 1)


def to_peer(value, mask):
    return lax.ppermute(value, PLANE, [(i, i ^ mask) for i in range(8)])


X_HOP, Y_HOP, XY_HOP, CORE_HOP = 4, 2, 6, 1


def along_shard(value, steps):
    count = lax.axis_size("shard")
    return lax.ppermute(value, "shard", [(i, (i + steps) % count) for i in range(count)])


def swap_ctx(value):
    return lax.ppermute(value, "ctx", [(0, 1), (1, 0)])


def in_order(first, own, other, axis):
    return jnp.where(
        first, jnp.concatenate([own, other], axis), jnp.concatenate([other, own], axis)
    )


def pick_half(first, value, axis):
    a, b = jnp.split(value, 2, axis=axis)
    return jnp.where(first, a, b), jnp.where(first, b, a)


def adam_update(weight, gradient, first_mom, second, step_rate, decay_here):
    moment = beta_first * first_mom + (1.0 - beta_first) * gradient
    square = beta_second * second + (1.0 - beta_second) * gradient * gradient
    ratio = (
        moment
        / (1.0 - beta_first**STEP)
        / (jnp.sqrt(square / (1.0 - beta_second**STEP)) + adam_eps)
    )
    new_weight = weight - step_rate * (ratio + decay_here * weight)
    return (moment, square, new_weight)


def norm_stats(values):
    row_mean = jnp.mean(values, axis=-1, keepdims=True)
    centred = values - row_mean
    row_var = jnp.mean(centred * centred, axis=-1, keepdims=True)
    return row_mean, lax.rsqrt(row_var + norm_eps)


def norm_back(grad, hat, scale, gain):
    scaled = grad * gain
    inner = jnp.mean(scaled * hat, axis=-1, keepdims=True)
    return scale * (scaled - jnp.mean(scaled, axis=-1, keepdims=True) - hat * inner)


BLOCK = 256


def dot_nt(a, b):
    return lax.dot_general(a, b, (((1,), (1,)), ((), ())), preferred_element_type=f32)


def dot_nn(a, b):
    return lax.dot_general(a, b, (((1,), (0,)), ((), ())), preferred_element_type=f32)


def dot_tn(a, b):
    return lax.dot_general(a, b, (((0,), (0,)), ((), ())), preferred_element_type=f32)


def block_of(rank, b):
    return pl.multiple_of(rel_of(b ^ rank) * 128, 128)


def score_pieces(nat, slope, head, at):
    lanes = pl.ds(head * HDIM, HDIM)
    query = nat[pl.ds(at * BLOCK, BLOCK), lanes] * low(HDIM**-0.5)
    pieces = []
    spans = ([(0, at * BLOCK)] if at else []) + [(at * BLOCK, BLOCK)]
    for start, size in spans:
        key = nat[pl.ds(start, size), pl.ds(128 + head * HDIM, HDIM)]
        raw = dot_nt(key, query)
        down = lax.broadcasted_iota(jnp.int32, (size, BLOCK), 0)
        raw = raw + slope * (down + (start - at * BLOCK)).astype(f32)
        if start == at * BLOCK:
            across = lax.broadcasted_iota(jnp.int32, (size, BLOCK), 1)
            raw = jnp.where(down <= across, raw, mask_value)
        pieces.append((start, size, key, raw))
    return query, pieces


smem = pl.BlockSpec(memory_space=pltpu.SMEM)
vmem = pl.BlockSpec(memory_space=pltpu.VMEM)


def shape(dims, dtype):
    return jax.ShapeDtypeStruct(dims, dtype)


def run(body, outs, args, scratch=(), flops=0, after=()):
    given, spare = len(args), len(after)

    def kernel(*refs):
        body(*refs[:given], *refs[given + spare :])

    moved = sum(a.size * a.dtype.itemsize for a in args) + sum(
        o.size * jnp.dtype(o.dtype).itemsize for o in outs
    )
    return pl.pallas_call(
        kernel,
        out_shape=tuple(outs),
        in_specs=[smem if a.ndim == 1 else vmem for a in args]
        + [pl.BlockSpec(memory_space=pl.ANY)] * spare,
        out_specs=tuple(vmem for _ in outs),
        scratch_shapes=list(scratch),
        compiler_params=pltpu.CompilerParams(vmem_limit_bytes=40 * 1024 * 1024),
        cost_estimate=pl.CostEstimate(flops=flops, bytes_accessed=moved, transcendentals=0),
    )(*args, *after)


RANK, CTX, ROW_Y, CORE, LIVE, BLOCKS = 0, 1, 2, 3, 4, 5


def feature_at(ints, k):
    return pl.multiple_of(ints[BLOCKS + k] * 256, 256)


def rows_of(ints, local, got, swapped, j):
    dc, dx, dy = j >> 2, (j >> 1) & 1, j & 1
    y, c = ints[ROW_Y] ^ dy, ints[CORE] ^ dc
    if dx == 0:
        return local[pl.ds(pl.multiple_of((y * 2 + c) * 128, 128), 128), :]
    there = pl.ds(pl.multiple_of(y * 128, 128), 128)
    return (swapped if dc else got)[there, :]


def pack_kernel(ints, qkv, out, up, down, own_a, send_a, own_b, send_b):
    ctx = ints[CTX]
    for mine, a, b in ((True, own_a, own_b), (False, send_a, send_b)):
        half = ctx if mine else 1 - ctx
        at = pl.ds(pl.multiple_of(half * 128, 128), 128)
        for i in range(3):
            a[:, pl.ds(i * 128, 128)] = qkv[i, :, at].astype(low)
        a[:, pl.ds(384, 128)] = out[at, :].astype(low)
        b[pl.ds(0, 128), :] = up[:, pl.ds(pl.multiple_of(half * 512, 512), 512)].astype(low)
        for i in range(4):
            tile = pl.ds(pl.multiple_of(half * 512 + i * 128, 128), 128)
            b[pl.ds(128, 128), pl.ds(i * 128, 128)] = down[tile, :].astype(low)


def norm_kernel(ints, vec, local, got, swapped, out):
    for j in range(8):
        values = rows_of(ints, local, got, swapped, j).astype(f32)
        mean, scale = norm_stats(values)
        out[pl.ds(j * 128, 128), :] = (
            (values - mean) * scale * vec[pl.ds(0, 1), :] + vec[pl.ds(1, 1), :]
        ).astype(low)


def mask_kernel(ints, local, got, swapped, out):
    for j in range(8):
        values = rows_of(ints, local, got, swapped, j)
        start = (ints[RANK] ^ mask_of(j)) * 128
        place = start + lax.broadcasted_iota(jnp.int32, values.shape, 0)
        out[pl.ds(j * 128, 128), :] = jnp.where(
            place < ints[LIVE], values.astype(f32), 0.0
        ).astype(low)


def out_kernel(ints, a0, a1, a2, a3, out):
    for k, a in enumerate((a0, a1, a2, a3)):
        for x in range(2):
            at = pl.multiple_of(ints[BLOCKS + k] * 256 + x * 128, 128)
            out[:, pl.ds(at, 128)] = a[pl.ds(x * 128, 128), pl.ds(384, 128)]


def attend_kernel(ints, slope_ref, vec, normed, a0, a1, a2, a3, qkv_ref, out_ref, top_ref, nat):
    rank, ctx = ints[RANK], ints[CTX]
    rows = normed.shape[0]
    part = rank - ctx * 4
    head_at = pl.ds(pl.multiple_of(part * 256 + ctx * 128, 128), 128)
    total = jnp.zeros((rows, 384), f32)
    for k, a in enumerate((a0, a1, a2, a3)):
        total = total + dot_nn(normed[:, pl.ds(feature_at(ints, k), 256)], a[:, pl.ds(0, 384)])
    for i, row in ((0, 2), (1, None), (2, 3)):
        some = total[:, i * 128 : (i + 1) * 128]
        if row is not None:
            some = some + vec[pl.ds(row, 1), head_at]
        qkv_ref[:, pl.ds(i * 128, 128)] = some.astype(low)
    for b in range(rows // 128):
        nat[pl.ds(b * 128, 128), :] = qkv_ref[pl.ds(block_of(rank, b), 128), :]
    for at in range(rows // BLOCK):
        outs = []
        for head in range(2):
            _, pieces = score_pieces(nat, slope_ref[head], head, at)
            top = functools.reduce(
                jnp.maximum, [jnp.max(raw, axis=0, keepdims=True) for _, _, _, raw in pieces]
            )
            probs = [jnp.exp(raw - top) for _, _, _, raw in pieces]
            total = sum(jnp.sum(p, axis=0, keepdims=True) for p in probs)
            inverse = 1.0 / total
            mixed = jnp.zeros((HDIM, BLOCK), f32)
            for (start, size, _, _), p in zip(pieces, probs):
                value = nat[pl.ds(start, size), pl.ds(256 + head * HDIM, HDIM)]
                mixed = mixed + dot_tn(value, (p * inverse).astype(low))
            outs.append(mixed.T)
            top_ref[pl.ds(head, 1), pl.ds(at * BLOCK, BLOCK)] = top + jnp.log(total)
        both = jnp.concatenate(outs, axis=1).astype(low)
        for part in range(BLOCK // 128):
            b = at * (BLOCK // 128) + part
            out_ref[pl.ds(block_of(rank, b), 128), :] = both[part * 128 : (part + 1) * 128]


def hidden_kernel(ints, vec, local, q0, q1, q2, q3, *refs):
    outs, (hidden, hat, scale_out, normed) = refs[:8], refs[8:]
    part = ints[RANK] - ints[CTX] * 4
    total = local[pl.ds(pl.multiple_of(part * 128, 128), 128), :].astype(f32)
    total = total + vec[pl.ds(4, 1), :]
    for c in range(2):
        for i, q in enumerate((q0, q1, q2, q3)):
            total = total + dot_nn(q[:, pl.ds(c * 128, 128)], outs[c * 4 + i][...])
    mean, scale = norm_stats(total)
    centred = (total - mean) * scale
    hidden[...] = total
    hat[...] = centred
    scale_out[...] = jnp.broadcast_to(scale, scale_out.shape)
    normed[...] = (centred * vec[pl.ds(5, 1), :] + vec[pl.ds(6, 1), :]).astype(low)


def unpack_up(ints, blocks, up):
    for k, b in enumerate(blocks):
        for x in range(2):
            at = pl.ds(pl.multiple_of(ints[BLOCKS + k] * 256 + x * 128, 128), 128)
            up[at, :] = b[pl.ds(x * 256, 128), :]


def unpack_down(ints, blocks, down):
    for k, b in enumerate(blocks):
        for x in range(2):
            at = pl.ds(pl.multiple_of(ints[BLOCKS + k] * 256 + x * 128, 128), 128)
            for i in range(4):
                down[pl.ds(i * 128, 128), at] = b[pl.ds(x * 256 + 128, 128), pl.ds(i * 128, 128)]


def forward_back_kernel(ints, vec, grad, *refs):
    normed, blocks = refs[:8], refs[8:12]
    act, up_grad, far, near, sums, whole, up, down = refs[12:]
    for j in range(8):
        whole[pl.ds(j * 128, 128), :] = normed[j][...]
    unpack_up(ints, blocks, up)
    unpack_down(ints, blocks, down)
    part = ints[RANK] - ints[CTX] * 4
    bias = vec[pl.ds(8 + part, 1), pl.ds(pl.multiple_of(ints[CTX] * 512, 512), 512)]
    coef = 0.7978845608028654
    bias_sum = jnp.zeros((1, 512), f32)
    for half in (1, 0):
        at = pl.ds(half * 512, 512)
        upward = dot_nn(whole[at, :], up[...]) + bias
        act_grad = dot_nt(grad[at, :], down[...])
        square = upward * upward
        tanh = jnp.tanh(coef * (upward + 0.044715 * square * upward))
        act[at, :] = (0.5 * upward * (1.0 + tanh)).astype(low)
        slope = 0.5 * (1.0 + tanh) + 0.5 * upward * (1.0 - tanh * tanh) * coef * (
            1.0 + 3.0 * 0.044715 * square
        )
        pre = (act_grad * slope).astype(low)
        up_grad[at, :] = pre
        bias_sum = bias_sum + jnp.sum(pre.astype(f32), axis=0, keepdims=True)
        back = dot_nt(pre, up[...])
        if half:
            far[...] = back.astype(low)
        else:
            near[...] = back
    sums[...] = bias_sum


def weight_grad_kernel(ints, grad, act, up_grad, *refs):
    normed, blocks = refs[:8], refs[8:12]
    g0, g1, g2, g3, far, near, whole, down = refs[12:]
    for j in range(8):
        whole[pl.ds(j * 128, 128), :] = normed[j][...]
    unpack_down(ints, blocks, down)
    for k, g in reversed(tuple(enumerate((g0, g1, g2, g3)))):
        at = pl.ds(feature_at(ints, k), 256)
        ups = dot_tn(whole[:, at], up_grad[...]).astype(low)
        downs = dot_tn(act[...], grad[:, at]).astype(low)
        for x in range(2):
            g[pl.ds(x * 256, 128), :] = ups[x * 128 : (x + 1) * 128]
            for i in range(4):
                g[pl.ds(x * 256 + 128, 128), pl.ds(i * 128, 128)] = downs[
                    i * 128 : (i + 1) * 128, x * 128 : (x + 1) * 128
                ]
    far[...] = dot_nn(act[pl.ds(512, 512), :], down[...]).astype(low)
    near[...] = dot_nn(act[pl.ds(0, 512), :], down[...])


def hidden_back_kernel(
    ints, vec, own, p0, p1, p2, hat, scale, grad, hidden_grad, attn_grad, sums
):
    total = own[...] + p0[...].astype(f32) + p1[...].astype(f32) + p2[...].astype(f32)
    hats = hat[...]
    live = grad[pl.ds(0, 128), :].astype(f32)
    back = live + norm_back(total, hats, scale[:, pl.ds(0, 1)], vec[pl.ds(5, 1), :])
    hidden_grad[...] = back
    rounded = back.astype(low)
    attn_grad[...] = rounded
    for i, value in enumerate((rounded.astype(f32), total * hats, total, live)):
        sums[pl.ds(i, 1), :] = jnp.sum(value, axis=0, keepdims=True)


def attend_back_kernel(ints, slope_ref, normed, qkv_ref, top_ref, context, out_weight, *refs):
    fulls, weights = refs[:8], refs[8:12]
    g0, g1, g2, g3, far, near, sums, nat, gnat, acc, rel, full = refs[12:]
    rank = ints[RANK]
    rows = qkv_ref.shape[0]
    for b in range(8):
        full[pl.ds(b * 128, 128), :] = fulls[b][...]
    heads = dot_nt(full[...], out_weight[...]).astype(low)
    for b in range(8):
        there = pl.multiple_of((rank ^ mask_of(b)) * 128, 128)
        gnat[pl.ds(there, 128), :] = heads[b * 128 : (b + 1) * 128]
    for b in range(rows // 128):
        nat[pl.ds(b * 128, 128), :] = qkv_ref[pl.ds(block_of(rank, b), 128), :]
    for head in range(2):
        for at in range(rows // BLOCK - 1, -1, -1):
            here = pl.ds(at * BLOCK, BLOCK)
            query, pieces = score_pieces(nat, slope_ref[head], head, at)
            grad = gnat[here, pl.ds(head * HDIM, HDIM)]
            log_total = top_ref[pl.ds(head, 1), here]
            probs, slopes = [], []
            inner = jnp.zeros((1, BLOCK), f32)
            for start, size, _, raw in pieces:
                value = nat[pl.ds(start, size), pl.ds(256 + head * HDIM, HDIM)]
                p = jnp.exp(raw - log_total)
                d = dot_nt(value, grad)
                inner = inner + jnp.sum(p * d, axis=0, keepdims=True)
                probs.append(p)
                slopes.append(d)
            query_grad = jnp.zeros((HDIM, BLOCK), f32)
            for (start, size, key, _), p, d in zip(pieces, probs, slopes):
                s = (p * (d - inner)).astype(low)
                query_grad = query_grad + dot_tn(key, s)
                key_grad = dot_nn(s, query)
                value_grad = dot_nn(p.astype(low), grad)
                k_at = (pl.ds(start, size), pl.ds(128 + head * HDIM, HDIM))
                v_at = (pl.ds(start, size), pl.ds(256 + head * HDIM, HDIM))
                if at == rows // BLOCK - 1:
                    acc[k_at] = key_grad
                    acc[v_at] = value_grad
                else:
                    acc[k_at] += key_grad
                    acc[v_at] += value_grad
            acc[here, pl.ds(head * HDIM, HDIM)] = query_grad.T * (HDIM**-0.5)
    bias_sum = jnp.zeros((1, 384), f32)
    for b in range(rows // 128):
        some = acc[pl.ds(b * 128, 128), :].astype(low)
        bias_sum = bias_sum + jnp.sum(some.astype(f32), axis=0, keepdims=True)
        rel[pl.ds(block_of(rank, b), 128), :] = some
    sums[...] = bias_sum
    for k in range(3, -1, -1):
        g, w = (g0, g1, g2, g3)[k], weights[k]
        at = pl.ds(feature_at(ints, k), 256)
        g[:, pl.ds(0, 384)] = dot_tn(normed[:, at], rel[...]).astype(low)
        outs = dot_tn(context[...], full[:, at]).astype(low)
        for x in range(2):
            g[pl.ds(x * 128, 128), pl.ds(384, 128)] = outs[:, x * 128 : (x + 1) * 128]
        far[:, at] = dot_nt(rel[pl.ds(512, 512), :], w[:, pl.ds(0, 384)]).astype(low)
        near[:, at] = dot_nt(rel[pl.ds(0, 512), :], w[:, pl.ds(0, 384)])


def last_kernel(ints, vec, local, own, p0, p1, p2, hidden_grad, wide, qkv_sums, up_sums, out, term):
    ctx = ints[CTX]
    part = ints[RANK] - ctx * 4
    values = local[pl.ds(pl.multiple_of(part * 128, 128), 128), :].astype(f32)
    mean, scale = norm_stats(values)
    hat = (values - mean) * scale
    total = own[...] + p0[...].astype(f32) + p1[...].astype(f32) + p2[...].astype(f32)
    out[...] = hidden_grad[...] + norm_back(total, hat, scale, vec[pl.ds(0, 1), :])
    term[...] = jnp.zeros_like(term)
    term[pl.ds(0, 1), :] = jnp.sum(total * hat, axis=0, keepdims=True)
    term[pl.ds(1, 1), :] = jnp.sum(total, axis=0, keepdims=True)
    head_at = pl.ds(pl.multiple_of(part * 256 + ctx * 128, 128), 128)
    term[pl.ds(2, 1), head_at] = qkv_sums[:, pl.ds(0, 128)]
    term[pl.ds(3, 1), head_at] = qkv_sums[:, pl.ds(256, 128)]
    term[pl.ds(4, 4), :] = wide[...]
    term[pl.ds(8 + part, 1), pl.ds(pl.multiple_of(ctx * 512, 512), 512)] = up_sums[...]


def add_kernel(ints, a, b, out):
    out[...] = (a[...].astype(f32) + b[...].astype(f32)).astype(out.dtype)


def adam_attn_kernel(ints, keep, got, qw, qf, qs, ow, of, os, qm, qq, qn, om, oq, on):
    ctx = ints[CTX]
    for source, half in ((keep, ctx), (got, 1 - ctx)):
        at = pl.ds(pl.multiple_of(half * 128, 128), 128)
        for i in range(3):
            g = source[:, pl.ds(i * 128, 128)].astype(f32)
            qm[i, :, at], qq[i, :, at], qn[i, :, at] = adam_update(
                qw[i, :, at], g, qf[i, :, at], qs[i, :, at], rate_matrix, decay_coef
            )
        g = source[:, pl.ds(384, 128)].astype(f32)
        om[at, :], oq[at, :], on[at, :] = adam_update(
            ow[at, :], g, of[at, :], os[at, :], rate_matrix, decay_coef
        )


def adam_ff_kernel(ints, keep, got, uw, uf, us, dw, df, ds, um, uq, un, dm, dq, dn):
    ctx = ints[CTX]
    for source, half in ((keep, ctx), (got, 1 - ctx)):
        at = pl.ds(pl.multiple_of(half * 512, 512), 512)
        g = source[pl.ds(0, 128), :].astype(f32)
        um[:, at], uq[:, at], un[:, at] = adam_update(
            uw[:, at], g, uf[:, at], us[:, at], rate_matrix, decay_coef
        )
        for i in range(4):
            tile = pl.ds(pl.multiple_of(half * 512 + i * 128, 128), 128)
            g = source[pl.ds(128, 128), pl.ds(i * 128, 128)].astype(f32)
            dm[tile, :], dq[tile, :], dn[tile, :] = adam_update(
                dw[tile, :], g, df[tile, :], ds[tile, :], rate_matrix, decay_coef
            )


def gather_blocks(block):
    quad = [block, to_peer(block, Y_HOP), to_peer(block, X_HOP), to_peer(block, XY_HOP)]
    return quad + [to_peer(one, CORE_HOP) for one in quad]


def scatter_halves(far, near):
    got = to_peer(far, CORE_HOP)
    quad = (near + got.astype(f32)).reshape(4, 128, -1)
    parts = quad[1:].astype(low)
    return (
        quad[0],
        to_peer(parts[0], Y_HOP),
        to_peer(parts[1], X_HOP),
        to_peer(parts[2], XY_HOP),
    )


def ring_blocks(block):
    blocks = [block]
    for _ in range(3):
        blocks.append(along_shard(blocks[-1], 1))
    return blocks


def ring_sum(blocks):
    total = blocks[3]
    for k in (2, 1, 0):
        total = along_shard(total, -1).astype(f32) + blocks[k].astype(f32)
        if k:
            total = total.astype(low)
    return total


def pack_attn(qkv, out):
    return [
        jnp.concatenate(
            [
                qkv[k * 256 : (k + 1) * 256],
                jnp.concatenate(jnp.split(out[:, k * 256 : (k + 1) * 256], 2, axis=1), axis=0),
            ],
            axis=1,
        )
        for k in range(4)
    ]


def unpack_attn(blocks):
    qkv = jnp.concatenate([b[:, :384] for b in blocks], axis=0)
    out = jnp.concatenate(
        [b[x * 128 : (x + 1) * 128, 384:] for b in blocks for x in range(2)], axis=1
    )
    return qkv, out


def pack_ff(up, down):
    blocks = []
    for k in range(4):
        parts = []
        for x in range(2):
            at = k * 256 + x * 128
            parts.append(up[at : at + 128])
            parts.append(
                jnp.concatenate(jnp.split(down[:, at : at + 128], 4, axis=0), axis=1)
            )
        blocks.append(jnp.concatenate(parts, axis=0))
    return blocks


def unpack_ff(blocks):
    ups, downs = [], []
    for b in blocks:
        for x in range(2):
            ups.append(b[x * 256 : x * 256 + 128])
            tiles = b[x * 256 + 128 : x * 256 + 256]
            downs.append(jnp.concatenate(jnp.split(tiles, 4, axis=1), axis=0))
    return jnp.concatenate(ups, axis=0), jnp.concatenate(downs, axis=1)


def per_device(
    tokens,
    cotangent,
    lengths,
    qkv_weight,
    out_weight,
    up_weight,
    down_weight,
    vectors,
    qkv_first,
    out_first,
    up_first,
    down_first,
    vec_first,
    qkv_second,
    out_second,
    up_second,
    down_second,
    vec_second,
):
    tok_rows, feat = tokens.shape
    shards = lax.axis_size("shard")
    ringed = feat // shards == 256
    ctx = lax.axis_index("ctx")
    part = lax.axis_index("tensor")
    place = lax.axis_index("shard")
    first = ctx == 0
    rank = ctx * 4 + part
    rows = 2 * tok_rows
    order = [lax.rem(place - k + shards, shards) if ringed else k for k in range(4)]
    ints = jnp.stack(
        [jnp.asarray(i, jnp.int32) for i in [rank, ctx, part // 2, part % 2, lengths[0]] + order]
    )

    if ringed:
        own_a, send_a, own_b, send_b = run(
            pack_kernel,
            [shape((128, 512), low)] * 2 + [shape((256, 512), low)] * 2,
            [ints, qkv_weight, out_weight, up_weight, down_weight],
        )
        block_a = in_order(first, own_a, swap_ctx(send_a), 0)
        attn_weights = ring_blocks(block_a)
    else:

        def fetch(weight, column_axis, feature_axis):
            own, send = pick_half(first, weight.astype(low), column_axis)
            whole = in_order(first, own, swap_ctx(send), feature_axis)
            return lax.all_gather(whole, "shard", axis=feature_axis, tiled=True)

        qkv_flat = jnp.concatenate(
            [qkv_weight[i][:, h * 128 : (h + 1) * 128] for h in range(2) for i in range(3)], axis=1
        )
        attn_weights = pack_attn(fetch(qkv_flat, 1, 0), fetch(out_weight, 0, 1))

    def other_rows(value):
        mine = value.reshape(2, 2, 128, feat)
        got = swap_ctx(
            lax.dynamic_index_in_dim(mine, part % 2, 1, keepdims=False).reshape(256, feat)
        )
        return got, to_peer(got, CORE_HOP)

    got, swapped = other_rows(tokens)
    every = lax.all_to_all(
        jnp.broadcast_to(vectors[None], (8 * shards,) + vectors.shape), ALL, 0, 0, tiled=True
    )
    vec = every.reshape(12, feat)
    normed_one = run(
        norm_kernel, [shape((rows, feat), low)], [ints, vec, tokens, got, swapped]
    )[0]

    if ringed:
        block_b = in_order(first, own_b, swap_ctx(send_b), 0)
        ff_weights = ring_blocks(block_b)
    else:
        ff_weights = pack_ff(fetch(up_weight, 1, 0), fetch(down_weight, 0, 1))

    out_local = run(out_kernel, [shape((128, feat), low)], [ints] + attn_weights)[0]
    out_blocks = gather_blocks(out_local)

    slopes_all = jnp.exp2(-8.0 * (jnp.arange(HEADS).astype(f32) + 1.0) / HEADS)
    slopes = lax.dynamic_slice_in_dim(slopes_all, part * 4 + ctx * 2, 2)
    qkv, context, tops = run(
        attend_kernel,
        [shape((rows, 384), low), shape((rows, 128), low), shape((8, rows), f32)],
        [ints, slopes, vec, normed_one] + attn_weights,
        [pltpu.VMEM((rows, 384), low)],
        flops=2 * rows * feat * 384 + 6 * rows * rows * HDIM,
    )

    cot_got, cot_swapped = other_rows(cotangent)
    out_grad = run(
        mask_kernel, [shape((rows, feat), low)], [ints, cotangent, cot_got, cot_swapped]
    )[0]

    blocks = context.reshape(2, 4, 128, 128)
    quad = jnp.concatenate([blocks[0], to_peer(blocks[1], CORE_HOP)], axis=2)
    quad = [quad[0], to_peer(quad[1], Y_HOP), to_peer(quad[2], X_HOP), to_peer(quad[3], XY_HOP)]
    hidden_rows, hat_two, scale_two, normed_own = run(
        hidden_kernel,
        [shape((128, feat), f32), shape((128, feat), f32), shape((128, 128), f32)]
        + [shape((128, feat), low)],
        [ints, vec, tokens] + quad + out_blocks,
        flops=2 * 128 * feat * feat,
    )
    normed_two = gather_blocks(normed_own)

    activated, up_grad, far, near, up_sums = run(
        forward_back_kernel,
        [shape((rows, 512), low)] * 2
        + [shape((512, feat), low), shape((512, feat), f32), shape((1, 512), f32)],
        [ints, vec, out_grad] + normed_two + ff_weights,
        [pltpu.VMEM((rows, feat), low), pltpu.VMEM((feat, 512), low), pltpu.VMEM((512, feat), low)],
        flops=6 * rows * feat * 512,
    )
    norm_two_parts = scatter_halves(far, near)
    *ff_grads, down_far, down_near = run(
        weight_grad_kernel,
        [shape((512, 512), low)] * 4 + [shape((512, feat), low), shape((512, feat), f32)],
        [ints, out_grad, activated, up_grad] + normed_two + ff_weights,
        [pltpu.VMEM((rows, feat), low), pltpu.VMEM((512, feat), low)],
        flops=6 * rows * feat * 512,
        after=[norm_two_parts[0]],
    )
    hidden_grad, attn_grad, wide = run(
        hidden_back_kernel,
        [shape((128, feat), f32), shape((128, feat), low), shape((4, feat), f32)],
        [ints, vec, *norm_two_parts, hat_two, scale_two, out_grad],
    )
    attn_grads = gather_blocks(attn_grad)
    *grads, far, near, qkv_sums = run(
        attend_back_kernel,
        [shape((256, 512), low)] * 4
        + [shape((512, feat), low), shape((512, feat), f32), shape((1, 384), f32)],
        [ints, slopes, normed_one, qkv, tops, context, out_local]
        + attn_grads
        + attn_weights,
        [
            pltpu.VMEM((rows, 384), low),
            pltpu.VMEM((rows, 128), low),
            pltpu.VMEM((rows, 384), f32),
            pltpu.VMEM((rows, 384), low),
            pltpu.VMEM((rows, feat), low),
        ],
        flops=15 * rows * rows * HDIM + 4 * rows * feat * 384 + 2 * rows * feat * 128,
    )
    norm_one_parts = scatter_halves(far, near)
    down_parts = scatter_halves(down_far, down_near)
    layer_out = (
        hidden_rows + vec[7:8] + sum(p.astype(f32) for p in down_parts)
    ).astype(low)

    attn_total = grads[3]
    if ringed:
        for k in (2, 1):
            attn_total = run(
                add_kernel,
                [shape((256, 512), low)],
                [ints, along_shard(attn_total, -1), grads[k]],
                after=[norm_one_parts[0]] if k == 2 else [],
            )[0]
    token_grad, term = run(
        last_kernel,
        [shape((128, feat), f32), shape((12, feat), f32)],
        [ints, vec, tokens, *norm_one_parts, hidden_grad, wide, qkv_sums, up_sums],
        after=[attn_total],
    )
    vector_grad = jnp.sum(
        lax.all_to_all(term.reshape((8 * shards,) + vectors.shape), ALL, 0, 0, tiled=True), axis=0
    )

    def settle(total):
        keep, send = pick_half(first, total, 0)
        return keep, swap_ctx(send.astype(low))

    if ringed:
        total = ff_grads[3]
        for k in (2, 1, 0):
            total = run(
                add_kernel,
                [shape(total.shape, low if k else f32)],
                [ints, along_shard(total, -1), ff_grads[k]],
                after=[] if k else [token_grad],
            )[0]
        keep_b, got_b = settle(total)
        total = run(
            add_kernel,
            [shape((256, 512), f32)],
            [ints, along_shard(attn_total, -1), grads[0]],
        )[0]
        keep_a, got_a = settle(total)
    else:

        def owned(total, column_axis, feature_axis):
            total = lax.psum_scatter(
                total.astype(f32), "shard", scatter_dimension=feature_axis, tiled=True
            )
            keep, send = pick_half(first, total, feature_axis)
            return in_order(first, keep, swap_ctx(send.astype(low)).astype(f32), column_axis)

        qkv_total, out_total = unpack_attn(grads)
        up_total, down_total = unpack_ff(ff_grads)
        qkv_total = jnp.split(qkv_total, 3, axis=1)
        qkv_owned = jnp.stack([owned(g, 1, 0) for g in qkv_total])
        out_owned = owned(out_total, 0, 1)
        up_owned = owned(up_total, 1, 0)
        down_owned = owned(down_total, 0, 1)

    if ringed:
        up_moment, up_square, up_new, down_moment, down_square, down_new = run(
            adam_ff_kernel,
            [shape(up_weight.shape, f32)] * 3 + [shape(down_weight.shape, f32)] * 3,
            [ints, keep_b, got_b, up_weight, up_first, up_second]
            + [down_weight, down_first, down_second],
        )
        qkv_moment, qkv_square, qkv_new, out_moment, out_square, out_new = run(
            adam_attn_kernel,
            [shape(qkv_weight.shape, f32)] * 3 + [shape(out_weight.shape, f32)] * 3,
            [ints, keep_a, got_a, qkv_weight, qkv_first, qkv_second]
            + [out_weight, out_first, out_second],
        )
    else:
        qkv_moment, qkv_square, qkv_new = adam_update(
            qkv_weight, qkv_owned, qkv_first, qkv_second, rate_matrix, decay_coef
        )
        out_moment, out_square, out_new = adam_update(
            out_weight, out_owned, out_first, out_second, rate_matrix, decay_coef
        )
        up_moment, up_square, up_new = adam_update(
            up_weight, up_owned, up_first, up_second, rate_matrix, decay_coef
        )
        down_moment, down_square, down_new = adam_update(
            down_weight, down_owned, down_first, down_second, rate_matrix, decay_coef
        )
    vec_moment, vec_square, vec_new = adam_update(
        vectors, vector_grad, vec_first, vec_second, rate_vector, 0.0
    )
    return (
        layer_out,
        token_grad,
        qkv_moment,
        out_moment,
        up_moment,
        down_moment,
        vec_moment,
        qkv_square,
        out_square,
        up_square,
        down_square,
        vec_square,
        qkv_new,
        out_new,
        up_new,
        down_new,
        vec_new,
    )


def solution(mesh):
    rows = P(("shard", "ctx"), None)
    shares = P(ALL, None)
    weights = (
        P(None, ("shard", "ctx"), "tensor"),
        P("tensor", ("shard", "ctx")),
        P(("shard", "ctx"), "tensor"),
        P("tensor", ("shard", "ctx")),
        P(ALL),
    )
    return jax.shard_map(
        per_device,
        mesh=mesh,
        in_specs=(rows, rows, P("shard")) + weights * 3,
        out_specs=(shares, shares) + weights * 3,
        check_vma=False,
    )
```
